256 devices in a mesh: dp: 4 (over y_hi, core), space: 64 (over y_lo, z, x).
Axes of the slice: x: 4, y: 4 (y_hi: 2, y_lo: 2; y = y_hi * 2 + y_lo), z: 8, core: 2. Of those that a mesh axis runs over, the one named last changes fastest.
Arguments:
- field: bfloat16 [4, 128, 64, 128, 128], P('dp', 'space'), may hold values from -6 to 6
- cotangent: bfloat16 [4, 128, 64, 128, 128], P('dp', 'space'), may hold values from -6 to 6
- mode_weight: bfloat16 [256, 16, 64, 64], P('space'), may hold values from -3 to 3
- point_weight: bfloat16 [64, 64], replicated, may hold values from -0.75 to 0.75
- point_bias: float32 [64], replicated, may hold values from -3 to 3
Outputs:
- field_grad: bfloat16 [4, 128, 64, 128, 128], P('dp', 'space')
- mode_grad: float32 [256, 16, 64, 64], P('space', 'dp')
The draws below stay inside these ranges and needn't reach their ends.
All inputs are finite; a program needn't handle non-finite values.
Results may differ from the reference program's by a relative error of at most 0.012.
Values may be sent and summed in bfloat16 or wider, within the bound.
No kernel may reach another device: no remote copies, remote signals or barrier semaphores. Data moves between devices by JAX's collectives and lax.ppermute only.
A program may use at most 128 MiB of HBM per device.

```python
import math
import jax
import jax.numpy as jnp
from jax import lax

C = 64
M = 16
NY = 128
NZ = 128
NX = 128
SAMPLES = 4
PAIRS = 256


def block_scale(key, shape, cuts, low, top_value):
    factor_of, own = 1.0, jax.random.fold_in(key, 6)
    for position, blocks in cuts:
        steps = jnp.exp(jax.random.uniform(jax.random.fold_in(own, position), (blocks,), jnp.float32, low / len(cuts), top_value / len(cuts)))
        factor_of = factor_of * jnp.repeat(steps, shape[position] // blocks).reshape([-1 if axis == position else 1 for axis in range(len(shape))])
    return factor_of


def noise(stream_key, shape, width, limit, split=(), kind=jnp.bfloat16):
    factor_of = block_scale(stream_key, shape, split, -0.22, 0.18) if split else 1.0
    values = jax.random.normal(stream_key, shape, jnp.float32) * width * factor_of
    return jnp.minimum(jnp.maximum(values, -limit), limit).astype(kind)


def setup_inputs(seed: int = 0) -> dict:
    keys = jax.random.split(jax.random.key(seed), 6)
    field = noise(keys[0], (SAMPLES, NX, C, NY, NZ), 1.0, 6.0, ((0, 4), (1, 64)))
    cotangent = noise(keys[1], (SAMPLES, NX, C, NY, NZ), 1.0, 6.0, ((0, 4), (1, 64)))
    mode_weight = noise(keys[2], (PAIRS, M, C, C), 0.5, 3.0, ((0, 64),))
    point_weight = noise(keys[3], (C, C), C ** -0.5, 0.75)
    point_bias = noise(keys[4], (C,), 0.5, 3.0, (), jnp.float32)
    return dict(field=field, cotangent=cotangent, mode_weight=mode_weight, point_weight=point_weight, point_bias=point_bias)


def basis(length, count):
    points = jnp.arange(length, dtype=jnp.int32)[:, None]
    order = jnp.arange(count, dtype=jnp.int32)[None, :]
    freq = (order + 1) // 2
    phase = (points * freq % length).astype(jnp.float32) * (2.0 * math.pi / length)
    cosine = jnp.logical_or(order % 2 == 1, order == 0)
    return jnp.where(cosine, jnp.cos(phase), jnp.sin(phase)) * math.sqrt(2.0 / length)

def activation(value):
    return jax.nn.gelu(value, approximate=True)

def reference(field, cotangent, mode_weight, point_weight, point_bias):
    pairs = M * M
    table_z = basis(NZ, M).astype(jnp.bfloat16)
    table_y = basis(NY, M)
    table_x = basis(NX, M)
    highest = lax.Precision.HIGHEST

    def to_modes(plane):
        along = jnp.dot(plane.reshape(C * NY, NZ), table_z, preferred_element_type=jnp.float32).reshape(C, NY, M)
        return jnp.einsum('cym,yn->cnm', along, table_y, precision=highest).reshape(C, pairs)

    def from_modes(coeffs):
        expanded = jnp.einsum('cnm,yn->cym', coeffs.reshape(C, M, M), table_y, precision=highest).astype(jnp.bfloat16)
        return jnp.dot(expanded.reshape(C * NY, M), table_z.T, preferred_element_type=jnp.float32).reshape(C, NY, NZ)

    def one_sample(grad_spec, inputs):
        sample, cotan = inputs
        planes = lax.map(to_modes, sample)
        spectrum = jnp.einsum('xcp,xm->pmc', planes, table_x, precision=highest).astype(jnp.bfloat16)
        mixed = jnp.einsum('pmi,pmio->pmo', spectrum.astype(jnp.float32), mode_weight.astype(jnp.float32))
        spatial = jnp.einsum('pmo,xm->xop', mixed, table_x, precision=highest)

        def forward_plane(pieces):
            plane, cot_plane, coeffs = pieces
            point = jnp.dot(point_weight.T, plane.reshape(C, NY * NZ), preferred_element_type=jnp.float32).reshape(C, NY, NZ)
            pre = from_modes(coeffs) + point + point_bias[:, None, None]
            unused, pull = jax.vjp(activation, pre)
            slope = pull(cot_plane.astype(jnp.float32))[0].astype(jnp.bfloat16)
            return (slope, to_modes(slope))
        slopes, grad_planes = lax.map(forward_plane, (sample, cotan, spatial))
        grad_hat = jnp.einsum('xcp,xm->pmc', grad_planes, table_x, precision=highest).astype(jnp.bfloat16)
        grad_spec = grad_spec + spectrum.astype(jnp.float32)[:, :, :, None] * grad_hat.astype(jnp.float32)[:, :, None, :]
        back = jnp.einsum('pmo,pmio->pmi', grad_hat.astype(jnp.float32), mode_weight.astype(jnp.float32))
        back_spatial = jnp.einsum('pmi,xm->xip', back, table_x, precision=highest)

        def backward_plane(pieces):
            slope, coeffs = pieces
            point = jnp.dot(point_weight, slope.reshape(C, NY * NZ), preferred_element_type=jnp.float32).reshape(C, NY, NZ)
            return (from_modes(coeffs) + point).astype(jnp.bfloat16)
        grads = lax.map(backward_plane, (slopes, back_spatial))
        return (grad_spec, grads)
    init = jnp.zeros((pairs, M, C, C), jnp.float32)
    mode_grad, field_grad = lax.scan(one_sample, init, (field, cotangent))
    return (field_grad, mode_grad)
```

```python
import math

import jax
import jax.numpy as jnp
import numpy as np
from jax import lax
from jax.experimental import pallas as pl
from jax.experimental.pallas import tpu as pltpu
from jax.sharding import PartitionSpec as P

BF = jnp.bfloat16
F32 = jnp.float32

C = 64
M = 16
N = 128
XL = 2
XC = XL * C
PAIRS = M * M
OWN = 4
GROUPS = 64
G = 16


def basis(length, count):
    points = np.arange(length)[:, None]
    order = np.arange(count)[None, :]
    freq = (order + 1) // 2
    phase = (points * freq % length).astype(np.float32) * np.float32(2.0 * math.pi / length)
    cosine = np.logical_or(order % 2 == 1, order == 0)
    table = np.where(cosine, np.cos(phase), np.sin(phase)) * np.float32(math.sqrt(2.0 / length))
    return table.astype(np.float32)


def split(table):
    high = table.astype(BF)
    return high, (table - high.astype(np.float32)).astype(BF)


def tables():
    base = basis(N, M)
    table_z = base.astype(BF)
    forward_y = np.concatenate([np.kron(np.eye(2, dtype=np.float32), part.astype(np.float32).T) for part in split(base)])
    back_y = np.concatenate(split(base), axis=1)
    by_plane = base.reshape(GROUPS, XL, M)
    along_x = np.einsum("sxm,pq->xpmsq", by_plane, np.eye(OWN, dtype=np.float32)).reshape(XL * OWN * M, GROUPS * OWN)
    back_z = np.kron(np.eye(M, dtype=np.float32), table_z.astype(np.float32).T)
    return dict(
        forward_y=forward_y.astype(BF),
        back_y=back_y.astype(BF),
        forward_z=np.ascontiguousarray(table_z.T),
        back_z=back_z.astype(BF),
        along_x=along_x,
        back_x=np.ascontiguousarray(along_x.T),
    )


def y_modes(group, forward_y, scratch, row):
    block = jnp.concatenate(
        [jnp.concatenate(group[0:2], axis=0), jnp.concatenate(group[2:4], axis=0)], axis=1
    )
    both = jnp.dot(forward_y, block, preferred_element_type=F32)
    modes = both[: 2 * M] + both[2 * M :]
    scratch[pl.ds(row, 2 * M), :] = modes[:, :N]
    scratch[pl.ds(row + 2 * M, 2 * M), :] = modes[:, N:]


def z_modes(scratch, forward_z, out_ref):
    for a in range(M):
        part = scratch[pl.ds(a, XC, stride=M), :].astype(BF)
        out_ref[M * a : M * (a + 1), :] = lax.dot_general(
            forward_z, part, (((1,), (1,)), ((), ())), preferred_element_type=F32
        ).astype(out_ref.dtype)


def from_z_modes(modes, back_z, scratch):
    wide = lax.dot_general(modes, back_z, (((0,), (0,)), ((), ())), preferred_element_type=F32)
    for a in range(M):
        scratch[pl.ds(a, XC, stride=M), :] = wide[:, N * a : N * (a + 1)]


def from_y_modes(scratch, back_y, row):
    pair = jnp.concatenate(
        [scratch[pl.ds(row, M), :].astype(BF), scratch[pl.ds(row + M, M), :].astype(BF)], axis=1
    )
    return jnp.dot(back_y, jnp.concatenate([pair, pair], axis=0), preferred_element_type=F32)


def to_modes_kernel(field_ref, forward_y_ref, forward_z_ref, out_ref, scratch):
    step = pl.program_id(0)
    for g in range(0, G, 4):
        group = [field_ref[g + k] for k in range(4)]
        y_modes(group, forward_y_ref[...], scratch, (step * G + g) * M)

    @pl.when(step == XC // G - 1)
    def _():
        z_modes(scratch, forward_z_ref[...], out_ref)


def slope_kernel(
    spatial_ref, back_z_ref, back_y_ref, forward_y_ref, forward_z_ref, point_ref, cot_ref,
    slope_ref, out_ref, spread, scratch,
):
    step = pl.program_id(0)
    root = math.sqrt(2.0 / math.pi)

    @pl.when(step == 0)
    def _():
        from_z_modes(spatial_ref[...], back_z_ref[...], spread)

    for g in range(0, G, 4):
        group = []
        for k in range(0, 4, 2):
            both = from_y_modes(spread, back_y_ref[...], (step * G + g + k) * M)
            for h in range(2):
                pre = both[:, N * h : N * (h + 1)] + point_ref[g + k + h].astype(F32)
                square = pre * pre
                tanh = jnp.tanh(pre * (root + (root * 0.044715) * square))
                outer = pre * (root + (root * 3 * 0.044715) * square)
                slope = (0.5 + 0.5 * tanh) * (1.0 + outer * (1.0 - tanh))
                slope = (slope * cot_ref[g + k + h].astype(F32)).astype(BF)
                slope_ref[g + k + h] = slope
                group.append(slope)
        y_modes(group, forward_y_ref[...], scratch, (step * G + g) * M)

    @pl.when(step == XC // G - 1)
    def _():
        z_modes(scratch, forward_z_ref[...], out_ref)


def result_kernel(back_ref, back_z_ref, back_y_ref, point_ref, out_ref, spread):
    step = pl.program_id(0)

    @pl.when(step == 0)
    def _():
        from_z_modes(back_ref[...], back_z_ref[...], spread)

    for g in range(0, G, 2):
        both = from_y_modes(spread, back_y_ref[...], (step * G + g) * M)
        for h in range(2):
            out_ref[g + h] = (both[:, N * h : N * (h + 1)] + point_ref[g + h].astype(F32)).astype(BF)


ROWS = 16
YB = 32


def point_kernel(weight_ref, spread_ref, bias_ref, in_ref, out_ref, wide):
    size = C * ROWS

    @pl.when(pl.program_id(0) == 0)
    def _():
        rows = jnp.dot(spread_ref[...], weight_ref[...], preferred_element_type=F32).astype(BF)
        for k in range(0, size, 256):
            all_of = lax.dot_general(
                rows[k : k + 256], spread_ref[...], (((1,), (1,)), ((), ())), preferred_element_type=F32
            )
            row = lax.broadcasted_iota(jnp.int32, (256, size), 0)
            column = lax.broadcasted_iota(jnp.int32, (256, size), 1)
            wide[k : k + 256, :] = jnp.where(row % ROWS == column % ROWS, all_of, 0.0).astype(BF)

    for y in range(0, YB, 2 * ROWS):
        block = jnp.concatenate(
            [in_ref[0, :, y + k * ROWS : y + (k + 1) * ROWS, :].reshape(size, N) for k in range(2)], axis=1
        )
        for k in range(0, size, 256):
            part = jnp.dot(wide[k : k + 256, :], block, preferred_element_type=F32)
            bias = bias_ref[k : k + 256, :]
            chan = k // ROWS
            for h in range(2):
                out_ref[0, chan : chan + 256 // ROWS, y + h * ROWS : y + (h + 1) * ROWS, :] = (
                    (part[:, N * h : N * (h + 1)] + bias).astype(BF).reshape(256 // ROWS, ROWS, N)
                )


def x_modes(received, along_x):
    both = jnp.dot(along_x, received.astype(F32), precision=lax.Precision.HIGHEST, preferred_element_type=F32)
    half = OWN * M
    lane = lax.broadcasted_iota(jnp.int32, (half, XC), 1)
    picked = jnp.where(lane < C, both[:half], both[half:])
    return picked + pltpu.roll(picked, C, 1)


def from_x_modes(twice, back_x):
    lane = lax.broadcasted_iota(jnp.int32, (OWN * M, XC), 1)
    stacked = jnp.concatenate([jnp.where(lane < C, twice, 0.0), jnp.where(lane < C, 0.0, twice)], axis=0)
    return jnp.dot(back_x, stacked, precision=lax.Precision.HIGHEST, preferred_element_type=F32)


def mix_kernel(received_ref, along_x_ref, back_x_ref, weight_ref, out_ref, spectrum_ref):
    spectrum = x_modes(received_ref[...], along_x_ref[...]).astype(BF)
    spectrum_ref[...] = spectrum
    lane = lax.broadcasted_iota(jnp.int32, (OWN * M, XC), 1)
    row = lax.broadcasted_iota(jnp.int32, (OWN * M, XC), 0) % M
    wide = spectrum.astype(F32)
    spread = jnp.concatenate(
        [jnp.where(lane // C + 2 * k == row, wide, 0.0).astype(BF) for k in range(M // 2)], axis=1
    )
    mixed = jnp.concatenate(
        [
            jnp.dot(spread[M * p : M * (p + 1)], weight_ref[p], preferred_element_type=F32)
            for p in range(OWN)
        ],
        axis=0,
    )
    twice = jnp.concatenate([mixed, mixed], axis=1)
    out_ref[...] = from_x_modes(twice, back_x_ref[...]).astype(out_ref.dtype)


def mix_back_kernel(received_ref, along_x_ref, back_x_ref, weight_ref, spectrum_ref, out_ref, both_ref):
    hat = x_modes(received_ref[...], along_x_ref[...]).astype(BF)
    lane = lax.broadcasted_iota(jnp.int32, (OWN * M, XC), 1)
    both_ref[...] = jnp.where(lane < C, spectrum_ref[...].astype(F32), hat.astype(F32)).astype(BF)
    lane = lax.broadcasted_iota(jnp.int32, (M, XC), 1)
    row = lax.broadcasted_iota(jnp.int32, (M, XC), 0)
    parts = []
    for p in range(OWN):
        every = lax.dot_general(
            hat[M * p : M * (p + 1), :C], weight_ref[p], (((1,), (1,)), ((), ())), preferred_element_type=F32
        )
        total = sum(
            jnp.where(lane // C + 2 * k == row, every[:, XC * k : XC * (k + 1)], 0.0) for k in range(M // 2)
        )
        parts.append(total + pltpu.roll(total, C, 1))
    out_ref[...] = from_x_modes(jnp.concatenate(parts, axis=0), back_x_ref[...]).astype(out_ref.dtype)


def whole(shape):
    return pl.BlockSpec(shape, lambda *unused: (0,) * len(shape))


def planes(*unused):
    return pl.BlockSpec((G, N, N), lambda i: (i, 0, 0))


def params(mib):
    return pltpu.CompilerParams(vmem_limit_bytes=mib * 1024 * 1024)


def cost(flops, size):
    return pl.CostEstimate(flops=flops, bytes_accessed=size, transcendentals=0)


BIG = jax.ShapeDtypeStruct((XC, N, N), BF)
SMALL = jax.ShapeDtypeStruct((PAIRS, XC), BF)
ALL_BYTES = XC * N * N * 2


def to_modes(field, table):
    return pl.pallas_call(
        to_modes_kernel,
        grid=(XC // G,),
        in_specs=[planes(), whole((4 * M, 2 * N)), whole((M, N))],
        out_specs=whole((PAIRS, XC)),
        out_shape=SMALL,
        scratch_shapes=[pltpu.VMEM((XC * M, N), F32)],
        compiler_params=params(60),
        cost_estimate=cost(XC * N * N * 128, ALL_BYTES),
        name="to_modes",
    )(field, table["forward_y"], table["forward_z"])


def slopes(spatial, point, cot, table):
    return pl.pallas_call(
        slope_kernel,
        grid=(XC // G,),
        in_specs=[
            whole((PAIRS, XC)), whole((PAIRS, M * N)), whole((N, 2 * M)), whole((4 * M, 2 * N)),
            whole((M, N)), planes(), planes(),
        ],
        out_specs=(planes(), whole((PAIRS, XC))),
        out_shape=(BIG, SMALL),
        scratch_shapes=[pltpu.VMEM((XC * M, N), F32)] * 2,
        compiler_params=params(60),
        cost_estimate=cost(XC * N * N * 256, 3 * ALL_BYTES),
        name="slopes",
    )(spatial, table["back_z"], table["back_y"], table["forward_y"], table["forward_z"], point, cot)


def result(back, point, table):
    return pl.pallas_call(
        result_kernel,
        grid=(XC // G,),
        in_specs=[whole((PAIRS, XC)), whole((PAIRS, M * N)), whole((N, 2 * M)), planes()],
        out_specs=planes(),
        out_shape=BIG,
        scratch_shapes=[pltpu.VMEM((XC * M, N), F32)],
        compiler_params=params(60),
        cost_estimate=cost(XC * N * N * 128, 2 * ALL_BYTES),
        name="result",
    )(back, table["back_z"], table["back_y"], point)


def pointwise(weight, bias, array):
    size = C * ROWS
    spread = np.kron(np.eye(C, dtype=np.float32), np.ones((ROWS, 1), np.float32)).astype(BF)
    rows = jnp.broadcast_to(bias[:, None, None], (C, ROWS, N)).reshape(size, N)
    block = pl.BlockSpec((1, C, YB, N), lambda i: (i // (N // YB), 0, i % (N // YB), 0))
    return pl.pallas_call(
        point_kernel,
        grid=(XL * (N // YB),),
        in_specs=[whole((C, C)), whole((size, C)), whole((size, N)), block],
        out_specs=block,
        out_shape=jax.ShapeDtypeStruct((XL, C, N, N), BF),
        scratch_shapes=[pltpu.VMEM((size, size), BF)],
        compiler_params=params(60),
        cost_estimate=cost(XC * N * N * 2048, 2 * ALL_BYTES),
        name="pointwise",
    )(weight, spread, rows, array.reshape(XL, C, N, N)).reshape(XC, N, N)


def mix(received, weight, table):
    return pl.pallas_call(
        mix_kernel,
        out_shape=(SMALL, jax.ShapeDtypeStruct((OWN * M, XC), BF)),
        compiler_params=params(60),
        cost_estimate=cost(1 << 27, 1 << 21),
        name="mix",
    )(received, table["along_x"], table["back_x"], weight)


def mix_back(received, weight, spectrum, table):
    return pl.pallas_call(
        mix_back_kernel,
        out_shape=(SMALL, jax.ShapeDtypeStruct((OWN * M, XC), BF)),
        compiler_params=params(60),
        cost_estimate=cost(1 << 27, 1 << 21),
        name="mix_back",
    )(received, table["along_x"], table["back_x"], weight, spectrum)


def exchange(array):
    cut = array.reshape(GROUPS, OWN, XC)
    return lax.all_to_all(cut, "space", split_axis=0, concat_axis=0, tiled=True).reshape(PAIRS, XC)


def per_device(field, cotangent, mode_weight, point_weight, point_bias):
    table = {name: jnp.asarray(value) for name, value in tables().items()}
    sample = field.reshape(XC, N, N)
    cot = cotangent.reshape(XC, N, N)
    weight = mode_weight.reshape(OWN, M * C, C)

    received = exchange(to_modes(sample, table))
    point = pointwise(point_weight.T, point_bias, sample)
    spatial, spectrum = mix(received, weight, table)
    slope, grad_modes = slopes(exchange(spatial), point, cot, table)
    received = exchange(grad_modes)
    point_back = pointwise(point_weight, jnp.zeros((C,), F32), slope)
    back, both = mix_back(received, weight, spectrum, table)
    back = exchange(back)
    every = lax.all_gather(both, "dp").reshape(4, OWN, M, 2, C)
    mine = lax.dynamic_slice_in_dim(every, lax.axis_index("dp") * (M // 4), M // 4, axis=2)
    mode_grad = jnp.einsum("spmi,spmo->pmio", mine[:, :, :, 0], mine[:, :, :, 1], preferred_element_type=F32)
    field_grad = result(back, point_back, table)
    return field_grad.reshape(1, XL, C, N, N), mode_grad


def solution(mesh):
    return jax.shard_map(
        per_device,
        mesh=mesh,
        in_specs=(
            P("dp", "space", None, None, None),
            P("dp", "space", None, None, None),
            P("space", None, None, None),
            P(),
            P(),
        ),
        out_specs=(P("dp", "space", None, None, None), P("space", "dp", None, None)),
        check_vma=False,
    )
```

```python
import functools
import math

import jax
import jax.numpy as jnp
import numpy as np
from jax import lax
from jax.experimental import pallas as pl
from jax.experimental.pallas import tpu as pltpu
from jax.sharding import PartitionSpec as P

BF = jnp.bfloat16
F32 = jnp.float32

C = 64
M = 16
N = 128
XL = 2
XC = XL * C
PAIRS = M * M
OWN = 4
GROUPS = 64
CHUNKS = 8
G = XC // CHUNKS


def basis(length, count):
    points = np.arange(length)[:, None]
    order = np.arange(count)[None, :]
    freq = (order + 1) // 2
    phase = (points * freq % length).astype(np.float32) * np.float32(2.0 * math.pi / length)
    cosine = np.logical_or(order % 2 == 1, order == 0)
    table = np.where(cosine, np.cos(phase), np.sin(phase)) * np.float32(math.sqrt(2.0 / length))
    return table.astype(np.float32)


def split(table):
    high = table.astype(BF)
    return high, (table - high.astype(np.float32)).astype(BF)


def tables():
    base = basis(N, M)
    table_z = base.astype(BF)
    forward_y = np.concatenate([np.kron(np.eye(2, dtype=np.float32), part.astype(np.float32).T) for part in split(base)])
    back_y = np.concatenate(split(base), axis=1)
    by_plane = base.reshape(GROUPS, XL, M)
    along_x = np.einsum("sxm,pq->xpmsq", by_plane, np.eye(OWN, dtype=np.float32)).reshape(XL * OWN * M, GROUPS * OWN)
    return dict(
        forward_y=forward_y.astype(BF),
        forward_y_half=(0.5 * forward_y).astype(BF),
        spread=np.kron(np.eye(C, dtype=np.float32), np.ones((ROWS, 1), np.float32)).astype(BF),
        back_y=back_y.astype(BF),
        forward_z=np.ascontiguousarray(table_z.T),
        along_x=along_x,
        back_x=np.ascontiguousarray(along_x.T),
    )


def y_modes(group, forward_y, scratch, row):
    block = jnp.concatenate(
        [jnp.concatenate(group[0:2], axis=0), jnp.concatenate(group[2:4], axis=0)], axis=1
    )
    both = jnp.dot(forward_y, block, preferred_element_type=F32)
    modes = both[: 2 * M] + both[2 * M :]
    scratch[pl.ds(row, 2 * M), :] = modes[:, :N]
    scratch[pl.ds(row + 2 * M, 2 * M), :] = modes[:, N:]


def z_modes(scratch, forward_z, out_ref):
    for a in range(M):
        part = scratch[pl.ds(a, XC, stride=M), :].astype(BF)
        out_ref[M * a : M * (a + 1), :] = lax.dot_general(
            forward_z, part, (((1,), (1,)), ((), ())), preferred_element_type=F32
        ).astype(out_ref.dtype)


def from_z_modes(modes, table_z, scratch):
    for a in range(M):
        scratch[pl.ds(a, XC, stride=M), :] = lax.dot_general(
            modes[M * a : M * (a + 1)], table_z, (((0,), (0,)), ((), ())), preferred_element_type=F32
        )


def from_y_modes(scratch, back_y, row):
    pair = jnp.concatenate(
        [scratch[pl.ds(row, M), :].astype(BF), scratch[pl.ds(row + M, M), :].astype(BF)], axis=1
    )
    return jnp.dot(back_y, jnp.concatenate([pair, pair], axis=0), preferred_element_type=F32)


def fetch(source, target, sems):
    return lambda k: pltpu.make_async_copy(
        source.at[pl.ds(G * k, G)], target.at[pl.ds(G * k, G)], sems.at[k]
    )


def fetch(source, target, sems, first=0):
    return lambda k: pltpu.make_async_copy(
        source.at[pl.ds(G * (k - first), G)], target.at[pl.ds(G * k, G)], sems.at[k]
    )


def fetch_planes(planes, target, sems):
    half = CHUNKS // XL
    copies = [fetch(source, target, sems, half * plane) for plane, source in enumerate(planes)]
    return lambda k: copies[k // half](k)


def to_modes_kernel(field_ref, forward_y_ref, forward_z_ref, out_ref, held, scratch, forward_y, forward_z, sems, own_sems):
    small = [
        pltpu.make_async_copy(forward_y_ref, forward_y, own_sems.at[0]),
        pltpu.make_async_copy(forward_z_ref, forward_z, own_sems.at[1]),
    ]
    copy = fetch(field_ref, held, sems)
    for each in small:
        each.start()
    for k in range(CHUNKS):
        copy(k).start()
    for each in small:
        each.wait()
    for k in range(CHUNKS):
        copy(k).wait()
        for g in range(G * k, G * (k + 1), 4):
            y_modes([held[g + j] for j in range(4)], forward_y[...], scratch, g * M)
    z_modes(scratch, forward_z[...], out_ref)


def doubled_slope(pre, cot):
    root = math.sqrt(2.0 / math.pi)
    square = pre * pre
    tanh = jnp.tanh(pre * (root + (root * 0.044715) * square))
    outer = pre * (root + (root * 3 * 0.044715) * square)
    return (1.0 + tanh) * (1.0 + outer * (1.0 - tanh)) * cot


def slope_kernel(
    spatial_ref, table_z_ref, back_y_ref, forward_y_ref, point0_ref, point1_ref, cot_ref,
    slope_ref, out_ref, spread, scratch, point, cot, slope, sems,
):
    point_copy = fetch_planes((point0_ref, point1_ref), point, sems.at[0])
    cot_copy = fetch(cot_ref, cot, sems.at[1])
    slope_copy = fetch(slope, slope_ref, sems.at[2])
    for k in range(CHUNKS):
        point_copy(k).start()
        cot_copy(k).start()
    from_z_modes(spatial_ref[...], table_z_ref[...], spread)
    last = None
    for first in range(0, XC, 4):
        if first % G == 0:
            point_copy(first // G).wait()
            cot_copy(first // G).wait()
        group = []
        for at in range(first, first + 4, 2):
            both = from_y_modes(spread, back_y_ref[...], at * M).astype(BF)
            for h in range(2):
                value = doubled_slope(both[:, N * h : N * (h + 1)] + point[at + h], cot[at + h])
                slope[at + h] = value
                group.append(value)
        if last is not None:
            y_modes(last, forward_y_ref[...], scratch, (first - 4) * M)
        last = group
        if first % G == G - 4:
            slope_copy(first // G).start()
    y_modes(last, forward_y_ref[...], scratch, (XC - 4) * M)
    z_modes(scratch, table_z_ref[...], out_ref)
    for k in range(CHUNKS):
        slope_copy(k).wait()


def result_kernel(
    back_ref, table_z_ref, back_y_ref, weight_ref, spread_ref, both0_ref, both1_ref, both2_ref, both3_ref,
    point0_ref, slope_ref, out_ref, mode_grad_ref, spread, point, slope, held, wide, grads, sems, row_sems,
):
    half = CHUNKS // XL
    point_copy = fetch(point0_ref, point, sems.at[0])
    out_copy = fetch(held, out_ref, sems.at[1])
    slope_copy = fetch_rows(slope_ref.at[pl.ds(C, C)], slope, row_sems)
    for k in range(half):
        point_copy(k).start()
    for k in range(STEPS):
        slope_copy(k).start()
    from_z_modes(back_ref[...], table_z_ref[...], spread)

    def finish(k):
        for g in range(G * k, G * (k + 1), 2):
            both = from_y_modes(spread, back_y_ref[...], g * M)
            for h in range(2):
                held[g + h] = (both[:, N * h : N * (h + 1)] + point[g + h].astype(F32)).astype(BF)
        out_copy(k).start()

    for k in range(half):
        point_copy(k).wait()
        finish(k)
    widen(weight_ref, spread_ref, wide, False, 0.5)
    for k in range(STEPS):
        slope_copy(k).wait()
        point_rows(slope, wide, None, point.at[pl.ds(C, C)], k)
    for k in range(half, CHUNKS):
        finish(k)
    mode_gradient((both0_ref, both1_ref, both2_ref, both3_ref), grads, mode_grad_ref)
    for k in range(CHUNKS):
        out_copy(k).wait()


def mode_gradient(samples, grads, out_ref):
    quarter = M // len(samples)
    own = lax.axis_index("dp") * quarter
    for s, ref in enumerate(samples):
        grads[s] = ref[...].astype(F32)
    lane = lax.broadcasted_iota(jnp.int32, (M, quarter * C), 1)
    row = lax.broadcasted_iota(jnp.int32, (M, quarter * C), 0)
    for p in range(OWN):
        rows = jnp.concatenate([grads[s, pl.ds(p * M + own, quarter), :] for s in range(len(samples))], axis=0)
        spectrum = jnp.concatenate([rows[:, :C]] * quarter, axis=1)
        spectrum = jnp.where(lane // C == row % quarter, spectrum, 0.0).astype(BF)
        out_ref[p] = lax.dot_general(
            spectrum, rows[:, C:].astype(BF), (((0,), (0,)), ((), ())), preferred_element_type=F32
        ).reshape(quarter, C, C)


ROWS = 8
WIDE = C * ROWS


def widen(weight_ref, spread_ref, wide, transposed, factor):
    rows = lax.dot_general(
        spread_ref[...], weight_ref[...], (((1,), (int(transposed),)), ((), ())), preferred_element_type=F32
    ).astype(BF)
    for k in range(0, WIDE, 128):
        every = lax.dot_general(
            rows[k : k + 128], spread_ref[...], (((1,), (1,)), ((), ())), preferred_element_type=F32
        )
        row = lax.broadcasted_iota(jnp.int32, (128, WIDE), 0)
        column = lax.broadcasted_iota(jnp.int32, (128, WIDE), 1)
        wide[k : k + 128, :] = jnp.where(row % ROWS == column % ROWS, every * factor, 0.0).astype(BF)


YB = 32
STEPS = N // YB


def fetch_rows(source, target, sems):
    def copy(k):
        at = (slice(None), pl.ds(k * YB, YB))
        return pltpu.make_async_copy(source.at[at], target.at[at], sems.at[k])

    return copy


def point_rows(array, wide, bias, out, k):
    size = 256
    for y in range(k * YB, (k + 1) * YB, 2 * ROWS):
        values = array[:, y : y + 2 * ROWS, :].astype(F32)
        block = jnp.concatenate(
            [values[:, ROWS * h : ROWS * (h + 1)].reshape(WIDE, N).astype(BF) for h in range(2)], axis=1
        )
        for at in range(0, WIDE, size):
            part = jnp.dot(wide[at : at + size, :], block, preferred_element_type=F32)
            pieces = []
            for h in range(2):
                piece = part[:, N * h : N * (h + 1)]
                if bias is not None:
                    piece = piece + bias[at : at + size, :]
                pieces.append(piece.reshape(size // ROWS, ROWS, N))
            out[at // ROWS : (at + size) // ROWS, y : y + 2 * ROWS, :] = jnp.concatenate(pieces, axis=1).astype(
                out.dtype
            )


def point_kernel(plane, back, weight_ref, spread_ref, *refs):
    (*bias_ref, in_ref, out_ref), (array, out, wide, bias, sems) = refs[:-5], refs[-5:]
    copy = fetch_rows(in_ref.at[pl.ds(plane * C, C)], array, sems.at[0])
    out_copy = fetch_rows(out, out_ref, sems.at[1])
    for k in range(STEPS):
        copy(k).start()
    if bias_ref:
        bias[...] = lax.dot_general(
            spread_ref[...].astype(F32), jnp.broadcast_to(bias_ref[0][...], (N, C)), (((1,), (1,)), ((), ())),
            precision=lax.Precision.HIGHEST, preferred_element_type=F32,
        )
    widen(weight_ref, spread_ref, wide, not back, 0.5 if back else 1.0)
    for k in range(STEPS):
        copy(k).wait()
        point_rows(array, wide, bias if bias_ref else None, out, k)
        out_copy(k).start()
    for k in range(STEPS):
        out_copy(k).wait()


def x_modes(received, along_x):
    both = jnp.dot(along_x, received.astype(F32), precision=lax.Precision.HIGHEST, preferred_element_type=F32)
    half = OWN * M
    lane = lax.broadcasted_iota(jnp.int32, (half, XC), 1)
    picked = jnp.where(lane < C, both[:half], both[half:])
    return picked + pltpu.roll(picked, C, 1)


def from_x_modes(twice, back_x):
    lane = lax.broadcasted_iota(jnp.int32, (OWN * M, XC), 1)
    stacked = jnp.concatenate([jnp.where(lane < C, twice, 0.0), jnp.where(lane < C, 0.0, twice)], axis=0)
    return jnp.dot(back_x, stacked, precision=lax.Precision.HIGHEST, preferred_element_type=F32)


def mix_kernel(received_ref, along_x_ref, back_x_ref, weight_ref, out_ref, spectrum_ref):
    spectrum = x_modes(received_ref[...], along_x_ref[...]).astype(BF)
    spectrum_ref[...] = spectrum
    lane = lax.broadcasted_iota(jnp.int32, (OWN * M, XC), 1)
    row = lax.broadcasted_iota(jnp.int32, (OWN * M, XC), 0) % M
    wide = spectrum.astype(F32)
    spread = jnp.concatenate(
        [jnp.where(lane // C + 2 * k == row, wide, 0.0).astype(BF) for k in range(M // 2)], axis=1
    )
    mixed = jnp.concatenate(
        [
            jnp.dot(spread[M * p : M * (p + 1)], weight_ref[p], preferred_element_type=F32)
            for p in range(OWN)
        ],
        axis=0,
    )
    twice = jnp.concatenate([mixed, mixed], axis=1)
    out_ref[...] = from_x_modes(twice, back_x_ref[...]).astype(out_ref.dtype)


def mix_back_kernel(received_ref, along_x_ref, back_x_ref, weight_ref, spectrum_ref, out_ref, both_ref):
    hat = x_modes(received_ref[...], along_x_ref[...]).astype(BF)
    lane = lax.broadcasted_iota(jnp.int32, (OWN * M, XC), 1)
    both_ref[...] = jnp.where(lane < C, spectrum_ref[...].astype(F32), hat.astype(F32)).astype(BF)
    lane = lax.broadcasted_iota(jnp.int32, (M, XC), 1)
    row = lax.broadcasted_iota(jnp.int32, (M, XC), 0)
    parts = []
    for p in range(OWN):
        every = lax.dot_general(
            hat[M * p : M * (p + 1), :C], weight_ref[p], (((1,), (1,)), ((), ())), preferred_element_type=F32
        )
        total = sum(
            jnp.where(lane // C + 2 * k == row, every[:, XC * k : XC * (k + 1)], 0.0) for k in range(M // 2)
        )
        parts.append(total + pltpu.roll(total, C, 1))
    out_ref[...] = from_x_modes(jnp.concatenate(parts, axis=0), back_x_ref[...]).astype(out_ref.dtype)


SMALL = pl.BlockSpec(memory_space=pltpu.VMEM)
LARGE = pl.BlockSpec(memory_space=pltpu.HBM)


def params(mib):
    return pltpu.CompilerParams(vmem_limit_bytes=mib * 1024 * 1024)


def cost(flops, size):
    return pl.CostEstimate(flops=flops, bytes_accessed=size, transcendentals=0)


ALL_BYTES = XC * N * N * 2
LARGE_OUT = pltpu.HBM((XC, N, N), BF)
PLANE_OUT = pltpu.HBM((C, N, N), BF)
MODES_OUT = jax.ShapeDtypeStruct((PAIRS, XC), BF)
OWN_OUT = jax.ShapeDtypeStruct((OWN * M, XC), BF)
WHOLE = pltpu.VMEM((XC, N, N), BF)
PLANE = pltpu.VMEM((C, N, N), BF)
SPREAD = pltpu.VMEM((XC * M, N), F32)


def large(array):
    return pltpu.with_memory_space_constraint(array, pltpu.HBM)


def sems(arrays, count):
    return pltpu.SemaphoreType.DMA((arrays, count))


def to_modes(field, table):
    small = (table["forward_y"], table["forward_z"])
    return pl.pallas_call(
        to_modes_kernel,
        in_specs=[LARGE] * 3,
        out_specs=SMALL,
        out_shape=MODES_OUT,
        scratch_shapes=[
            WHOLE, SPREAD, *[pltpu.VMEM(each.shape, BF) for each in small],
            pltpu.SemaphoreType.DMA((CHUNKS,)), pltpu.SemaphoreType.DMA((2,)),
        ],
        compiler_params=params(40),
        cost_estimate=cost(XC * N * N * 128, ALL_BYTES),
        name="to_modes",
    )(large(field), *map(large, small))


def slopes(spatial, points, cot, table):
    return pl.pallas_call(
        slope_kernel,
        in_specs=[SMALL] * 4 + [LARGE] * 3,
        out_specs=(LARGE, SMALL),
        out_shape=(LARGE_OUT, MODES_OUT),
        scratch_shapes=[SPREAD] * 2 + [WHOLE] * 3 + [sems(3, CHUNKS)],
        compiler_params=params(40),
        cost_estimate=cost(XC * N * N * 256, 3 * ALL_BYTES),
        name="slopes",
    )(
        spatial, table["forward_z"], table["back_y"], table["forward_y_half"], *map(large, points), large(cot),
    )


def result(back, weight, samples, point0, slope, table):
    return pl.pallas_call(
        result_kernel,
        in_specs=[SMALL] * 9 + [LARGE] * 2,
        out_specs=(LARGE, SMALL),
        out_shape=(LARGE_OUT, jax.ShapeDtypeStruct((OWN, M // 4, C, C), F32)),
        scratch_shapes=[
            SPREAD, WHOLE, PLANE, WHOLE, pltpu.VMEM((WIDE, WIDE), BF), pltpu.VMEM((4, OWN * M, XC), F32),
            sems(2, CHUNKS), pltpu.SemaphoreType.DMA((STEPS,)),
        ],
        compiler_params=params(40),
        cost_estimate=cost(XC * N * N * 512, 2 * ALL_BYTES),
        name="result",
    )(
        back, table["forward_z"], table["back_y"], weight, table["spread"], *samples, large(point0), large(slope)
    )


def pointwise(plane, back, weight, bias, array, table):
    operands = [weight, table["spread"]] + ([] if back else [bias.reshape(1, C)])
    return pl.pallas_call(
        functools.partial(point_kernel, plane, back),
        in_specs=[SMALL] * len(operands) + [LARGE],
        out_specs=LARGE,
        out_shape=PLANE_OUT,
        scratch_shapes=[
            PLANE, PLANE, pltpu.VMEM((WIDE, WIDE), BF), pltpu.VMEM((WIDE, N), F32), sems(2, STEPS),
        ],
        compiler_params=params(40),
        cost_estimate=cost(C * N * N * 1024, ALL_BYTES),
        name="pointwise",
    )(*operands, large(array))


def mix(received, weight, table):
    return pl.pallas_call(
        mix_kernel,
        in_specs=[SMALL] * 4,
        out_specs=(SMALL, SMALL),
        out_shape=(MODES_OUT, OWN_OUT),
        compiler_params=params(40),
        cost_estimate=cost(1 << 27, 1 << 21),
        name="mix",
    )(received, table["along_x"], table["back_x"], weight)


def mix_back(received, weight, spectrum, table):
    return pl.pallas_call(
        mix_back_kernel,
        in_specs=[SMALL] * 5,
        out_specs=(SMALL, SMALL),
        out_shape=(MODES_OUT, OWN_OUT),
        compiler_params=params(40),
        cost_estimate=cost(1 << 27, 1 << 21),
        name="mix_back",
    )(received, table["along_x"], table["back_x"], weight, spectrum)


def exchange(array):
    cut = array.reshape(GROUPS, OWN, XC)
    return lax.all_to_all(cut, "space", split_axis=0, concat_axis=0, tiled=True).reshape(PAIRS, XC)


def over_samples(both):
    return [both] + [lax.ppermute(both, "dp", [(i, (i + k) % 4) for i in range(4)]) for k in range(1, 4)]


def per_device(field, cotangent, mode_weight, point_weight, point_bias):
    table = {name: jnp.asarray(value) for name, value in tables().items()}
    sample = field.reshape(XC, N, N)
    cot = cotangent.reshape(XC, N, N)
    weight = mode_weight.reshape(OWN, M * C, C)

    modes, sample = lax.optimization_barrier((to_modes(sample, table), sample))
    received = exchange(modes)
    point0 = pointwise(0, False, point_weight, point_bias, sample, table)
    received, point0 = lax.optimization_barrier((received, point0))
    spatial, spectrum = mix(received, weight, table)
    later, spatial = lax.optimization_barrier((sample, spatial))
    received = exchange(spatial)
    point1 = pointwise(1, False, point_weight, point_bias, later, table)
    slope, grad_modes = slopes(received, (point0, point1), cot, table)
    received = exchange(grad_modes)
    point_back0 = pointwise(0, True, point_weight, None, slope, table)
    received, point_back0 = lax.optimization_barrier((received, point_back0))
    back, both = mix_back(received, weight, spectrum, table)
    field_grad, mode_grad = result(exchange(back), point_weight, over_samples(both), point_back0, slope, table)
    return field_grad.reshape(1, XL, C, N, N), mode_grad


def solution(mesh):
    return jax.shard_map(
        per_device,
        mesh=mesh,
        in_specs=(
            P("dp", "space", None, None, None),
            P("dp", "space", None, None, None),
            P("space", None, None, None),
            P(),
            P(),
        ),
        out_specs=(P("dp", "space", None, None, None), P("space", "dp", None, None)),
        check_vma=False,
    )
```

```python
import functools
import math

import jax
import jax.numpy as jnp
import numpy as np
from jax import lax
from jax.experimental import pallas as pl
from jax.experimental.pallas import tpu as pltpu
from jax.sharding import PartitionSpec as P

BF = jnp.bfloat16
F32 = jnp.float32

C = 64
M = 16
N = 128
XL = 2
XC = XL * C
PAIRS = M * M
OWN = 4
GROUPS = 64
SLOPE_HEAD = 16
RESULT_HEAD = 32


def basis(length, count):
    points = np.arange(length)[:, None]
    order = np.arange(count)[None, :]
    freq = (order + 1) // 2
    phase = (points * freq % length).astype(np.float32) * np.float32(2.0 * math.pi / length)
    cosine = np.logical_or(order % 2 == 1, order == 0)
    table = np.where(cosine, np.cos(phase), np.sin(phase)) * np.float32(math.sqrt(2.0 / length))
    return table.astype(np.float32)


def split(table):
    high = table.astype(BF)
    return high, (table - high.astype(np.float32)).astype(BF)


def tables():
    base = basis(N, M)
    table_z = base.astype(BF)
    forward_y = np.concatenate([np.kron(np.eye(2, dtype=np.float32), part.astype(np.float32).T) for part in split(base)])
    back_y = np.concatenate(split(base), axis=1)
    by_plane = base.reshape(GROUPS, XL, M)
    along_x = np.einsum("sxm,pq->xpmsq", by_plane, np.eye(OWN, dtype=np.float32)).reshape(XL * OWN * M, GROUPS * OWN)
    return dict(
        forward_y=forward_y.astype(BF),
        forward_y_half=(0.5 * forward_y).astype(BF),
        spread=np.kron(np.eye(C, dtype=np.float32), np.ones((ROWS, 1), np.float32)).astype(BF),
        back_y=back_y.astype(BF),
        forward_z=np.ascontiguousarray(table_z.T),
        along_x=np.stack(split(along_x)),
        back_x=np.stack(split(np.ascontiguousarray(along_x.T))),
    )


def y_modes(group, forward_y, scratch, row):
    block = jnp.concatenate(
        [jnp.concatenate(group[0:2], axis=0), jnp.concatenate(group[2:4], axis=0)], axis=1
    )
    both = jnp.dot(forward_y, block, preferred_element_type=F32)
    modes = both[: 2 * M] + both[2 * M :]
    scratch[pl.ds(row, 2 * M), :] = modes[:, :N]
    scratch[pl.ds(row + 2 * M, 2 * M), :] = modes[:, N:]


def z_modes(scratch, forward_z, out_ref):
    for a in range(M):
        part = scratch[pl.ds(a, XC, stride=M), :].astype(BF)
        out_ref[M * a : M * (a + 1), :] = lax.dot_general(
            forward_z, part, (((1,), (1,)), ((), ())), preferred_element_type=F32
        ).astype(out_ref.dtype)


def from_z_modes(modes, table_z, scratch):
    for a in range(M):
        scratch[pl.ds(a, XC, stride=M), :] = lax.dot_general(
            modes[M * a : M * (a + 1)], table_z, (((0,), (0,)), ((), ())), preferred_element_type=F32
        )


def from_y_modes(scratch, back_y, row):
    pair = jnp.concatenate(
        [scratch[pl.ds(row, M), :].astype(BF), scratch[pl.ds(row + M, M), :].astype(BF)], axis=1
    )
    return jnp.dot(back_y, jnp.concatenate([pair, pair], axis=0), preferred_element_type=F32)


def pieces(source, target, sems, cuts, first=0):
    return {
        low: pltpu.make_async_copy(
            source.at[pl.ds(low - first, high - low)], target.at[pl.ds(low, high - low)], sems.at[k]
        )
        for k, (low, high) in enumerate(zip(cuts, cuts[1:]))
    }


FIELD_CUTS = (0, 48, 96, 128)


def to_modes_kernel(
    field_ref, forward_y_ref, forward_z_ref, out_ref, held, scratch, forward_y, forward_z, sems, small_sems
):
    small = [
        pltpu.make_async_copy(forward_y_ref, forward_y, small_sems.at[0]),
        pltpu.make_async_copy(forward_z_ref, forward_z, small_sems.at[1]),
    ]
    copies = pieces(field_ref, held, sems, FIELD_CUTS)
    for copy in (*small, *copies.values()):
        copy.start()
    for copy in small:
        copy.wait()
    for g in range(0, XC, 4):
        if g in copies:
            copies[g].wait()
        y_modes([held[g + j] for j in range(4)], forward_y[...], scratch, g * M)
    z_modes(scratch, forward_z[...], out_ref)


SLOPE_CUTS = (0, SLOPE_HEAD, 40, C, 96, 128)
SLOPE_OUT_CUTS = (0, 32, 64, 96, 112, 128)
RESULT_CUTS = (0, RESULT_HEAD, C, 96, 112, 128)


def doubled_slope(pre, cot):
    root = math.sqrt(2.0 / math.pi)
    square = pre * pre
    tanh = jnp.tanh(pre * (root + (root * 0.044715) * square))
    outer = pre * (root + (root * 3 * 0.044715) * square)
    return (1.0 + tanh) * (1.0 + outer * (1.0 - tanh)) * cot


def slope_kernel(
    spatial_ref, table_z_ref, back_y_ref, forward_y_ref, point_head_ref, cot_head_ref,
    point0_ref, point1_ref, cot_ref, slope_ref, out_ref, spread, scratch, point, cot, slope, sems,
):
    point_copies = pieces(point0_ref, point, sems.at[0], SLOPE_CUTS[1:4])
    point_copies |= pieces(point1_ref, point, sems.at[1], SLOPE_CUTS[3:], C)
    cot_copies = pieces(cot_ref, cot, sems.at[2], SLOPE_CUTS[1:])
    slope_copies = pieces(slope, slope_ref, sems.at[3], SLOPE_OUT_CUTS)
    for low in SLOPE_CUTS[1:-1]:
        point_copies[low].start()
        cot_copies[low].start()
    from_z_modes(spatial_ref[...], table_z_ref[...], spread)
    last = None
    for first in range(0, XC, 4):
        if first in cot_copies:
            point_copies[first].wait()
            cot_copies[first].wait()
        point_at, cot_at = (point, cot) if first >= SLOPE_HEAD else (point_head_ref, cot_head_ref)
        group = []
        for at in range(first, first + 4, 2):
            both = from_y_modes(spread, back_y_ref[...], at * M).astype(BF)
            for h in range(2):
                value = doubled_slope(both[:, N * h : N * (h + 1)] + point_at[at + h], cot_at[at + h])
                slope[at + h] = value
                group.append(value)
        if last is not None:
            y_modes(last, forward_y_ref[...], scratch, (first - 4) * M)
        last = group
        for low, high in zip(SLOPE_OUT_CUTS, SLOPE_OUT_CUTS[1:]):
            if first + 4 == high:
                slope_copies[low].start()
    y_modes(last, forward_y_ref[...], scratch, (XC - 4) * M)
    z_modes(scratch, table_z_ref[...], out_ref)
    for copy in slope_copies.values():
        copy.wait()


def result_kernel(
    back_ref, table_z_ref, back_y_ref, wide_ref, both0_ref, both1_ref, both2_ref, both3_ref, head_ref,
    point0_ref, slope_ref, out_ref, mode_grad_ref, spread, point, slope, held, grads, sems, row_sems,
):
    (point_copy,) = pieces(point0_ref, point, sems.at[0], (RESULT_HEAD, C)).values()
    out_copies = pieces(held, out_ref, sems.at[1], RESULT_CUTS)
    slope_copy = fetch_rows(slope_ref.at[pl.ds(C, C)], slope, row_sems, 2 * YB)
    point_copy.start()
    for k in range(STEPS // 2):
        slope_copy(k).start()
    from_z_modes(back_ref[...], table_z_ref[...], spread)

    def finish(low, high):
        for g in range(low, high, 2):
            both = from_y_modes(spread, back_y_ref[...], g * M)
            for h in range(2):
                other = head_ref[g + h] if g < RESULT_HEAD else point[g + h]
                held[g + h] = (both[:, N * h : N * (h + 1)] + other.astype(F32)).astype(BF)
        out_copies[low].start()

    for low, high in zip(RESULT_CUTS, RESULT_CUTS[1:]):
        if low == RESULT_HEAD:
            point_copy.wait()
        if low == C:
            for k in range(STEPS // 2):
                slope_copy(k).wait()
                point_rows(slope, wide_ref, None, point.at[pl.ds(C, C)], k, 2 * YB)
        finish(low, high)
    mode_gradient((both0_ref, both1_ref, both2_ref, both3_ref), grads, mode_grad_ref)
    for copy in out_copies.values():
        copy.wait()


def mode_gradient(samples, grads, out_ref):
    quarter = M // len(samples)
    own = lax.axis_index("dp") * quarter
    for s, ref in enumerate(samples):
        grads[s] = ref[...].astype(F32)
    lane = lax.broadcasted_iota(jnp.int32, (M, quarter * C), 1)
    row = lax.broadcasted_iota(jnp.int32, (M, quarter * C), 0)
    for p in range(OWN):
        rows = jnp.concatenate([grads[s, pl.ds(p * M + own, quarter), :] for s in range(len(samples))], axis=0)
        spectrum = jnp.concatenate([rows[:, :C]] * quarter, axis=1)
        spectrum = jnp.where(lane // C == row % quarter, spectrum, 0.0).astype(BF)
        out_ref[p] = lax.dot_general(
            spectrum, rows[:, C:].astype(BF), (((0,), (0,)), ((), ())), preferred_element_type=F32
        ).reshape(quarter, C, C)


ROWS = 8
WIDE = C * ROWS


def widen(weight_ref, spread_ref, wide, transposed, factor):
    rows = lax.dot_general(
        spread_ref[...], weight_ref[...], (((1,), (int(transposed),)), ((), ())), preferred_element_type=F32
    ).astype(BF)
    for k in range(0, WIDE, 128):
        every = lax.dot_general(
            rows[k : k + 128], spread_ref[...], (((1,), (1,)), ((), ())), preferred_element_type=F32
        )
        row = lax.broadcasted_iota(jnp.int32, (128, WIDE), 0)
        column = lax.broadcasted_iota(jnp.int32, (128, WIDE), 1)
        wide[k : k + 128, :] = jnp.where(row % ROWS == column % ROWS, every * factor, 0.0).astype(BF)


YB = 32
STEPS = N // YB


def fetch_rows(source, target, sems, count=YB):
    def copy(k):
        at = (slice(None), pl.ds(k * count, count))
        return pltpu.make_async_copy(source.at[at], target.at[at], sems.at[k])

    return copy


def point_rows(array, wide, bias, out, k, count=YB):
    size = 256
    for y in range(k * count, (k + 1) * count, 2 * ROWS):
        values = array[:, y : y + 2 * ROWS, :].astype(F32)
        block = jnp.concatenate(
            [values[:, ROWS * h : ROWS * (h + 1)].reshape(WIDE, N).astype(BF) for h in range(2)], axis=1
        )
        for at in range(0, WIDE, size):
            part = jnp.dot(wide[at : at + size, :], block, preferred_element_type=F32)
            pieces = []
            for h in range(2):
                piece = part[:, N * h : N * (h + 1)]
                if bias is not None:
                    piece = piece + bias[at : at + size, :]
                pieces.append(piece.reshape(size // ROWS, ROWS, N))
            out[at // ROWS : (at + size) // ROWS, y : y + 2 * ROWS, :] = jnp.concatenate(pieces, axis=1).astype(
                out.dtype
            )


def point_kernel(plane, back, weight_ref, spread_ref, *refs):
    refs, (array, out, bias, sems, head_sem) = refs[:-5], refs[-5:]
    if back:
        in_ref, out_ref, head_ref, wide = refs
    elif plane:
        bias_ref, in_ref, out_ref, wide = refs
    else:
        bias_ref, cot_ref, in_ref, out_ref, head_ref, cot_head_ref, wide = refs
    copy = fetch_rows(in_ref.at[pl.ds(plane * C, C)], array, sems.at[0])
    out_copy = fetch_rows(out, out_ref, sems.at[1])
    for k in range(STEPS):
        copy(k).start()
    if not back and not plane:
        head_copy = pltpu.make_async_copy(cot_ref.at[pl.ds(0, SLOPE_HEAD)], cot_head_ref, head_sem)
        head_copy.start()
    if not back:
        bias[...] = lax.dot_general(
            spread_ref[...].astype(F32), jnp.broadcast_to(bias_ref[...], (N, C)), (((1,), (1,)), ((), ())),
            precision=lax.Precision.HIGHEST, preferred_element_type=F32,
        )
    widen(weight_ref, spread_ref, wide, not back, 0.5 if back else 1.0)
    for k in range(STEPS):
        copy(k).wait()
        point_rows(array, wide, None if back else bias, out, k)
        out_copy(k).start()
    if not plane:
        head_ref[...] = out[: head_ref.shape[0]]
    for k in range(STEPS):
        out_copy(k).wait()
    if not back and not plane:
        head_copy.wait()


def x_modes(received, along_x):
    both = jnp.dot(along_x[0], received, preferred_element_type=F32)
    both += jnp.dot(along_x[1], received, preferred_element_type=F32)
    half = OWN * M
    lane = lax.broadcasted_iota(jnp.int32, (half, XC), 1)
    picked = jnp.where(lane < C, both[:half], both[half:])
    return picked + pltpu.roll(picked, C, 1)


def from_x_modes(twice, back_x):
    lane = lax.broadcasted_iota(jnp.int32, (OWN * M, XC), 1)
    stacked = jnp.concatenate([jnp.where(lane < C, twice, 0.0), jnp.where(lane < C, 0.0, twice)], axis=0)
    stacked = stacked.astype(BF)
    return jnp.dot(back_x[0], stacked, preferred_element_type=F32) + jnp.dot(
        back_x[1], stacked, preferred_element_type=F32
    )


def mix_kernel(received_ref, along_x_ref, back_x_ref, weight_ref, out_ref, spectrum_ref):
    spectrum = x_modes(received_ref[...], along_x_ref[...]).astype(BF)
    spectrum_ref[...] = spectrum
    lane = lax.broadcasted_iota(jnp.int32, (OWN * M, XC), 1)
    row = lax.broadcasted_iota(jnp.int32, (OWN * M, XC), 0) % M
    wide = spectrum.astype(F32)
    spread = jnp.concatenate(
        [jnp.where(lane // C + 2 * k == row, wide, 0.0).astype(BF) for k in range(M // 2)], axis=1
    )
    mixed = jnp.concatenate(
        [
            jnp.dot(spread[M * p : M * (p + 1)], weight_ref[p], preferred_element_type=F32)
            for p in range(OWN)
        ],
        axis=0,
    )
    twice = jnp.concatenate([mixed, mixed], axis=1)
    out_ref[...] = from_x_modes(twice, back_x_ref[...]).astype(out_ref.dtype)


def mix_back_kernel(received_ref, along_x_ref, back_x_ref, weight_ref, spectrum_ref, out_ref, both_ref):
    hat = x_modes(received_ref[...], along_x_ref[...]).astype(BF)
    lane = lax.broadcasted_iota(jnp.int32, (OWN * M, XC), 1)
    both_ref[...] = jnp.where(lane < C, spectrum_ref[...].astype(F32), hat.astype(F32)).astype(BF)
    lane = lax.broadcasted_iota(jnp.int32, (M, XC), 1)
    row = lax.broadcasted_iota(jnp.int32, (M, XC), 0)
    parts = []
    for p in range(OWN):
        every = lax.dot_general(
            hat[M * p : M * (p + 1), :C], weight_ref[p], (((1,), (1,)), ((), ())), preferred_element_type=F32
        )
        total = sum(
            jnp.where(lane // C + 2 * k == row, every[:, XC * k : XC * (k + 1)], 0.0) for k in range(M // 2)
        )
        parts.append(total + pltpu.roll(total, C, 1))
    out_ref[...] = from_x_modes(jnp.concatenate(parts, axis=0), back_x_ref[...]).astype(out_ref.dtype)


SMALL = pl.BlockSpec(memory_space=pltpu.VMEM)
LARGE = pl.BlockSpec(memory_space=pltpu.HBM)


def params(mib):
    return pltpu.CompilerParams(vmem_limit_bytes=mib * 1024 * 1024)


def cost(flops, size):
    return pl.CostEstimate(flops=flops, bytes_accessed=size, transcendentals=0)


ALL_BYTES = XC * N * N * 2
LARGE_OUT = pltpu.HBM((XC, N, N), BF)
PLANE_OUT = pltpu.HBM((C, N, N), BF)
MODES_OUT = jax.ShapeDtypeStruct((PAIRS, XC), BF)
OWN_OUT = jax.ShapeDtypeStruct((OWN * M, XC), BF)
WHOLE = pltpu.VMEM((XC, N, N), BF)
PLANE = pltpu.VMEM((C, N, N), BF)
SPREAD = pltpu.VMEM((XC * M, N), F32)


def large(array):
    return pltpu.with_memory_space_constraint(array, pltpu.HBM)


def sems(arrays, count):
    return pltpu.SemaphoreType.DMA((arrays, count))


def to_modes(field, table):
    small = (table["forward_y"], table["forward_z"])
    return pl.pallas_call(
        to_modes_kernel,
        in_specs=[LARGE] * 3,
        out_specs=SMALL,
        out_shape=MODES_OUT,
        scratch_shapes=[
            WHOLE, SPREAD, *[pltpu.VMEM(each.shape, BF) for each in small],
            pltpu.SemaphoreType.DMA((len(FIELD_CUTS) - 1,)), pltpu.SemaphoreType.DMA((2,)),
        ],
        compiler_params=params(40),
        cost_estimate=cost(XC * N * N * 128, ALL_BYTES),
        name="to_modes",
    )(large(field), *map(large, small))


def slopes(spatial, heads, points, cot, table):
    return pl.pallas_call(
        slope_kernel,
        in_specs=[SMALL] * 6 + [LARGE] * 3,
        out_specs=(LARGE, SMALL),
        out_shape=(LARGE_OUT, MODES_OUT),
        scratch_shapes=[SPREAD] * 2 + [WHOLE] * 3 + [sems(4, len(SLOPE_OUT_CUTS))],
        compiler_params=params(40),
        cost_estimate=cost(XC * N * N * 256, 3 * ALL_BYTES),
        name="slopes",
    )(
        spatial, table["forward_z"], table["back_y"], table["forward_y_half"], *heads,
        *map(large, points), large(cot),
    )


def result(back, wide, samples, head, point0, slope, table):
    return pl.pallas_call(
        result_kernel,
        in_specs=[SMALL] * 9 + [LARGE] * 2,
        out_specs=(LARGE, SMALL),
        out_shape=(LARGE_OUT, jax.ShapeDtypeStruct((OWN, M // 4, C, C), F32)),
        scratch_shapes=[
            SPREAD, WHOLE, PLANE, WHOLE, pltpu.VMEM((4, OWN * M, XC), F32),
            sems(2, len(RESULT_CUTS)), pltpu.SemaphoreType.DMA((STEPS,)),
        ],
        compiler_params=params(40),
        cost_estimate=cost(XC * N * N * 512, 2 * ALL_BYTES),
        name="result",
    )(
        back, table["forward_z"], table["back_y"], wide, *samples, head, large(point0), large(slope)
    )


def pointwise(plane, back, weight, bias, array, table, cot=None):
    operands = [weight, table["spread"]] + ([] if back else [bias.reshape(1, C)])
    sources = ([] if cot is None else [cot]) + [array]
    wide = pltpu.VMEM((WIDE, WIDE), BF)
    head = pltpu.VMEM((RESULT_HEAD if back else SLOPE_HEAD, N, N), BF)
    kept = [head] * (0 if plane else 1 + (cot is not None)) + [wide] * back
    return pl.pallas_call(
        functools.partial(point_kernel, plane, back),
        in_specs=[SMALL] * len(operands) + [LARGE] * len(sources),
        out_specs=[LARGE] + [SMALL] * len(kept),
        out_shape=[PLANE_OUT] + kept,
        scratch_shapes=[wide] * (not back)
        + [PLANE, PLANE, pltpu.VMEM((WIDE, N), F32), sems(2, STEPS), pltpu.SemaphoreType.DMA],
        compiler_params=params(40),
        cost_estimate=cost(C * N * N * 1024, ALL_BYTES),
        name="pointwise",
    )(*operands, *map(large, sources))


def mix(received, weight, table):
    return pl.pallas_call(
        mix_kernel,
        in_specs=[SMALL] * 4,
        out_specs=(SMALL, SMALL),
        out_shape=(MODES_OUT, OWN_OUT),
        compiler_params=params(40),
        cost_estimate=cost(1 << 27, 1 << 21),
        name="mix",
    )(received, table["along_x"], table["back_x"], weight)


def mix_back(received, weight, spectrum, table):
    return pl.pallas_call(
        mix_back_kernel,
        in_specs=[SMALL] * 5,
        out_specs=(SMALL, SMALL),
        out_shape=(MODES_OUT, OWN_OUT),
        compiler_params=params(40),
        cost_estimate=cost(1 << 27, 1 << 21),
        name="mix_back",
    )(received, table["along_x"], table["back_x"], weight, spectrum)


def exchange(array):
    cut = array.reshape(GROUPS, OWN, XC)
    return lax.all_to_all(cut, "space", split_axis=0, concat_axis=0, tiled=True).reshape(PAIRS, XC)


def over_samples(both):
    return [both] + [lax.ppermute(both, "dp", [(i, i ^ k) for i in range(4)]) for k in range(1, 4)]


def per_device(field, cotangent, mode_weight, point_weight, point_bias):
    table = {name: jnp.asarray(value) for name, value in tables().items()}
    sample = field.reshape(XC, N, N)
    cot = cotangent.reshape(XC, N, N)
    weight = mode_weight.reshape(OWN, M * C, C)

    modes, sample = lax.optimization_barrier((to_modes(sample, table), sample))
    received = exchange(modes)
    point0, *heads = pointwise(0, False, point_weight, point_bias, sample, table, cot)
    received, point0 = lax.optimization_barrier((received, point0))
    spatial, spectrum = mix(received, weight, table)
    later, spatial = lax.optimization_barrier((sample, spatial))
    received = exchange(spatial)
    (point1,) = pointwise(1, False, point_weight, point_bias, later, table)
    slope, grad_modes = slopes(received, heads, (point0, point1), cot, table)
    received = exchange(grad_modes)
    point_back0, head, wide = pointwise(0, True, point_weight, None, slope, table)
    received, point_back0 = lax.optimization_barrier((received, point_back0))
    back, both = mix_back(received, weight, spectrum, table)
    field_grad, mode_grad = result(
        exchange(back), wide, over_samples(both), head, point_back0, slope, table
    )
    return field_grad.reshape(1, XL, C, N, N), mode_grad


def solution(mesh):
    return jax.shard_map(
        per_device,
        mesh=mesh,
        in_specs=(
            P("dp", "space", None, None, None),
            P("dp", "space", None, None, None),
            P("space", None, None, None),
            P(),
            P(),
        ),
        out_specs=(P("dp", "space", None, None, None), P("space", "dp", None, None)),
        check_vma=False,
    )
```

```python
import functools
import math

import jax
import jax.numpy as jnp
import numpy as np
from jax import lax
from jax.experimental import pallas as pl
from jax.experimental.pallas import tpu as pltpu
from jax.sharding import PartitionSpec as P

BF = jnp.bfloat16
F32 = jnp.float32

C = 64
M = 16
N = 128
XL = 2
XC = XL * C
PAIRS = M * M
OWN = 4
GROUPS = 64
SLOPE_HEAD = 16
RESULT_HEAD = 32


def basis(length, count):
    points = np.arange(length)[:, None]
    order = np.arange(count)[None, :]
    freq = (order + 1) // 2
    phase = (points * freq % length).astype(np.float32) * np.float32(2.0 * math.pi / length)
    cosine = np.logical_or(order % 2 == 1, order == 0)
    table = np.where(cosine, np.cos(phase), np.sin(phase)) * np.float32(math.sqrt(2.0 / length))
    return table.astype(np.float32)


def split(table):
    high = table.astype(BF)
    return high, (table - high.astype(np.float32)).astype(BF)


def tables():
    base = basis(N, M)
    table_z = base.astype(BF)
    forward_y = np.concatenate([np.kron(np.eye(2, dtype=np.float32), part.astype(np.float32).T) for part in split(base)])
    back_y = np.concatenate(split(base), axis=1)
    by_plane = base.reshape(GROUPS, XL, M)
    along_x = np.einsum("sxm,pq->xpmsq", by_plane, np.eye(OWN, dtype=np.float32)).reshape(XL * OWN * M, GROUPS * OWN)
    return dict(
        forward_y=forward_y.astype(BF),
        forward_y_half=(0.5 * forward_y).astype(BF),
        spread=np.kron(np.eye(C, dtype=np.float32), np.ones((ROWS, 1), np.float32)).astype(BF),
        back_y=back_y.astype(BF),
        forward_z=np.ascontiguousarray(table_z.T),
        along_x=np.stack(split(along_x)),
        back_x=np.stack(split(np.ascontiguousarray(along_x.T))),
    )


def y_modes(group, forward_y, scratch, row):
    block = jnp.concatenate(
        [jnp.concatenate(group[0:2], axis=0), jnp.concatenate(group[2:4], axis=0)], axis=1
    )
    both = jnp.dot(forward_y, block, preferred_element_type=F32)
    modes = both[: 2 * M] + both[2 * M :]
    scratch[pl.ds(row, 2 * M), :] = modes[:, :N]
    scratch[pl.ds(row + 2 * M, 2 * M), :] = modes[:, N:]


def z_modes(scratch, forward_z, modes, out_ref, sem):
    for a in range(M):
        part = scratch[pl.ds(a, XC, stride=M), :].astype(BF)
        modes[M * a : M * (a + 1), :] = lax.dot_general(
            forward_z, part, (((1,), (1,)), ((), ())), preferred_element_type=F32
        ).astype(BF)
    copy = pltpu.make_async_copy(modes, out_ref, sem)
    copy.start()
    return copy


def from_z_modes(modes, table_z, scratch):
    for a in range(M):
        scratch[pl.ds(a, XC, stride=M), :] = lax.dot_general(
            modes[M * a : M * (a + 1)], table_z, (((0,), (0,)), ((), ())), preferred_element_type=F32
        )


def from_y_modes(scratch, back_y, row):
    pair = jnp.concatenate(
        [scratch[pl.ds(row, M), :].astype(BF), scratch[pl.ds(row + M, M), :].astype(BF)], axis=1
    )
    return jnp.dot(back_y, jnp.concatenate([pair, pair], axis=0), preferred_element_type=F32)


def pieces(source, target, sems, cuts, first=0):
    return {
        low: pltpu.make_async_copy(
            source.at[pl.ds(low - first, high - low)], target.at[pl.ds(low, high - low)], sems.at[k]
        )
        for k, (low, high) in enumerate(zip(cuts, cuts[1:]))
    }


FIELD_CUTS = (0, 48, 96, 128)


def to_modes_kernel(
    field_ref, forward_y_ref, forward_z_ref, out_ref, held, scratch, modes, forward_y, forward_z, sems, small_sems
):
    small = [
        pltpu.make_async_copy(forward_y_ref, forward_y, small_sems.at[0]),
        pltpu.make_async_copy(forward_z_ref, forward_z, small_sems.at[1]),
    ]
    copies = pieces(field_ref, held, sems, FIELD_CUTS)
    for copy in (*small, *copies.values()):
        copy.start()
    for copy in small:
        copy.wait()
    for g in range(0, XC, 4):
        if g in copies:
            copies[g].wait()
        y_modes([held[g + j] for j in range(4)], forward_y[...], scratch, g * M)
    z_modes(scratch, forward_z[...], modes, out_ref, small_sems.at[2]).wait()


SLOPE_CUTS = (0, SLOPE_HEAD, 40, C, 96, 128)
SLOPE_OUT_CUTS = (0, 32, 64, 88, 104, 116, 128)
RESULT_CUTS = (0, RESULT_HEAD, C, 96, 112, 128)
AHEAD = 2
BEHIND = 2


def ahead_of(product, count):
    ready = {}

    def take(at):
        for each in range(at, min(at + 2 * count + 2, XC), 2):
            if each not in ready:
                ready[each] = product(each)
        return ready[at]

    return take


def doubled_slope(pre, cot):
    root = math.sqrt(2.0 / math.pi)
    square = pre * pre
    tanh = jnp.tanh(pre * (root + (root * 0.044715) * square))
    outer = pre * (root + (root * 3 * 0.044715) * square)
    return (1.0 + tanh) * (1.0 + outer * (1.0 - tanh)) * cot


def slope_kernel(
    spatial_ref, table_z_ref, back_y_ref, forward_y_ref, point_head_ref, cot_head_ref,
    point0_ref, point1_ref, cot_ref, slope_ref, out_ref, spread, scratch, modes, point, cot, slope, sems, out_sem,
):
    point_copies = pieces(point0_ref, point, sems.at[0], SLOPE_CUTS[1:4])
    point_copies |= pieces(point1_ref, point, sems.at[1], SLOPE_CUTS[3:], C)
    cot_copies = pieces(cot_ref, cot, sems.at[2], SLOPE_CUTS[1:])
    slope_copies = pieces(slope, slope_ref, sems.at[3], SLOPE_OUT_CUTS)
    for low in SLOPE_CUTS[1:-1]:
        point_copies[low].start()
        cot_copies[low].start()
    from_z_modes(spatial_ref[...], table_z_ref[...], spread)
    spectral = ahead_of(lambda at: from_y_modes(spread, back_y_ref[...], at * M).astype(BF), AHEAD)
    waiting = []
    for first in range(0, XC, 4):
        if first in cot_copies:
            point_copies[first].wait()
            cot_copies[first].wait()
        point_at, cot_at = (point, cot) if first >= SLOPE_HEAD else (point_head_ref, cot_head_ref)
        group = []
        for at in range(first, first + 4, 2):
            both = spectral(at)
            for h in range(2):
                value = doubled_slope(both[:, N * h : N * (h + 1)] + point_at[at + h], cot_at[at + h])
                slope[at + h] = value
                group.append(value)
        waiting.append((group, first))
        if len(waiting) > BEHIND:
            group, row = waiting.pop(0)
            y_modes(group, forward_y_ref[...], scratch, row * M)
        for low, high in zip(SLOPE_OUT_CUTS, SLOPE_OUT_CUTS[1:]):
            if first + 4 == high:
                slope_copies[low].start()
    for group, row in waiting:
        y_modes(group, forward_y_ref[...], scratch, row * M)
    out_copy = z_modes(scratch, table_z_ref[...], modes, out_ref, out_sem)
    for copy in (*slope_copies.values(), out_copy):
        copy.wait()


def result_kernel(
    back_ref, table_z_ref, back_y_ref, wide_ref, both0_ref, both1_ref, both2_ref, both3_ref, head_ref,
    point0_ref, slope_ref, out_ref, mode_grad_ref, spread, point, slope, held, grads, total, sems, row_sems, sem,
):
    (point_copy,) = pieces(point0_ref, point, sems.at[0], (RESULT_HEAD, C)).values()
    out_copies = pieces(held, out_ref, sems.at[1], RESULT_CUTS)
    slope_copy = fetch_rows(slope_ref.at[pl.ds(C, C)], slope, row_sems, 2 * YB)
    point_copy.start()
    for k in range(STEPS // 2):
        slope_copy(k).start()
    mode_gradient((both0_ref, both1_ref, both2_ref, both3_ref), grads, total)
    mode_copy = pltpu.make_async_copy(total, mode_grad_ref, sem)
    mode_copy.start()
    from_z_modes(back_ref[...], table_z_ref[...], spread)

    spectral = ahead_of(lambda at: from_y_modes(spread, back_y_ref[...], at * M), 1)

    def finish(low, high):
        for g in range(low, high, 2):
            both = spectral(g)
            for h in range(2):
                other = head_ref[g + h] if g < RESULT_HEAD else point[g + h]
                held[g + h] = (both[:, N * h : N * (h + 1)] + other.astype(F32)).astype(BF)
        out_copies[low].start()

    for low, high in zip(RESULT_CUTS, RESULT_CUTS[1:]):
        if low == RESULT_HEAD:
            point_copy.wait()
        if low == C:
            for k in range(STEPS // 2):
                slope_copy(k).wait()
                point_rows(slope, wide_ref, None, point.at[pl.ds(C, C)], k, 2 * YB)
        finish(low, high)
    for copy in (*out_copies.values(), mode_copy):
        copy.wait()


def mode_gradient(samples, grads, out_ref):
    quarter = M // len(samples)
    own = lax.axis_index("dp") * quarter
    for s, ref in enumerate(samples):
        grads[s] = ref[...].astype(F32)
    lane = lax.broadcasted_iota(jnp.int32, (M, quarter * C), 1)
    row = lax.broadcasted_iota(jnp.int32, (M, quarter * C), 0)
    for p in range(OWN):
        rows = jnp.concatenate([grads[s, pl.ds(p * M + own, quarter), :] for s in range(len(samples))], axis=0)
        spectrum = jnp.concatenate([rows[:, :C]] * quarter, axis=1)
        spectrum = jnp.where(lane // C == row % quarter, spectrum, 0.0).astype(BF)
        out_ref[p] = lax.dot_general(
            spectrum, rows[:, C:].astype(BF), (((0,), (0,)), ((), ())), preferred_element_type=F32
        ).reshape(quarter, C, C)


ROWS = 8
WIDE = C * ROWS


def widen(weight_ref, spread_ref, wide, transposed, factor):
    rows = lax.dot_general(
        spread_ref[...], weight_ref[...], (((1,), (int(transposed),)), ((), ())), preferred_element_type=F32
    ).astype(BF)
    for k in range(0, WIDE, 128):
        every = lax.dot_general(
            rows[k : k + 128], spread_ref[...], (((1,), (1,)), ((), ())), preferred_element_type=F32
        )
        row = lax.broadcasted_iota(jnp.int32, (128, WIDE), 0)
        column = lax.broadcasted_iota(jnp.int32, (128, WIDE), 1)
        wide[k : k + 128, :] = jnp.where(row % ROWS == column % ROWS, every * factor, 0.0).astype(BF)


YB = 32
STEPS = N // YB


def fetch_rows(source, target, sems, count=YB):
    def copy(k):
        at = (slice(None), pl.ds(k * count, count))
        return pltpu.make_async_copy(source.at[at], target.at[at], sems.at[k])

    return copy


def point_rows(array, wide, bias, out, k, count=YB):
    size = 256
    for y in range(k * count, (k + 1) * count, 2 * ROWS):
        values = array[:, y : y + 2 * ROWS, :].astype(F32)
        block = jnp.concatenate(
            [values[:, ROWS * h : ROWS * (h + 1)].reshape(WIDE, N).astype(BF) for h in range(2)], axis=1
        )
        for at in range(0, WIDE, size):
            part = jnp.dot(wide[at : at + size, :], block, preferred_element_type=F32)
            pieces = []
            for h in range(2):
                piece = part[:, N * h : N * (h + 1)]
                if bias is not None:
                    piece = piece + bias[at : at + size, :]
                pieces.append(piece.reshape(size // ROWS, ROWS, N))
            out[at // ROWS : (at + size) // ROWS, y : y + 2 * ROWS, :] = jnp.concatenate(pieces, axis=1).astype(
                out.dtype
            )


def point_kernel(plane, back, weight_ref, spread_ref, *refs):
    refs, (array, out, bias, sems, head_sem) = refs[:-5], refs[-5:]
    if back:
        in_ref, out_ref, head_ref, wide = refs
    elif plane:
        bias_ref, in_ref, out_ref, wide = refs
    else:
        bias_ref, cot_ref, in_ref, out_ref, head_ref, cot_head_ref, wide = refs
    copy = fetch_rows(in_ref.at[pl.ds(plane * C, C)], array, sems.at[0])
    out_copy = fetch_rows(out, out_ref, sems.at[1])
    for k in range(STEPS):
        copy(k).start()
    if not back and not plane:
        head_copy = pltpu.make_async_copy(cot_ref.at[pl.ds(0, SLOPE_HEAD)], cot_head_ref, head_sem)
        head_copy.start()
    if not back:
        bias[...] = lax.dot_general(
            spread_ref[...].astype(F32), jnp.broadcast_to(bias_ref[...], (N, C)), (((1,), (1,)), ((), ())),
            precision=lax.Precision.HIGHEST, preferred_element_type=F32,
        )
    widen(weight_ref, spread_ref, wide, not back, 0.5 if back else 1.0)
    for k in range(STEPS):
        copy(k).wait()
        point_rows(array, wide, None if back else bias, out, k)
        out_copy(k).start()
    if not plane:
        head_ref[...] = out[: head_ref.shape[0]]
    for k in range(STEPS):
        out_copy(k).wait()
    if not back and not plane:
        head_copy.wait()


def x_modes(received, along_x):
    both = jnp.dot(along_x[0], received, preferred_element_type=F32)
    both += jnp.dot(along_x[1], received, preferred_element_type=F32)
    half = OWN * M
    lane = lax.broadcasted_iota(jnp.int32, (half, XC), 1)
    picked = jnp.where(lane < C, both[:half], both[half:])
    return picked + pltpu.roll(picked, C, 1)


def from_x_modes(twice, back_x):
    lane = lax.broadcasted_iota(jnp.int32, (OWN * M, XC), 1)
    stacked = jnp.concatenate([jnp.where(lane < C, twice, 0.0), jnp.where(lane < C, 0.0, twice)], axis=0)
    stacked = stacked.astype(BF)
    return jnp.dot(back_x[0], stacked, preferred_element_type=F32) + jnp.dot(
        back_x[1], stacked, preferred_element_type=F32
    )


def mix_kernel(received_ref, along_x_ref, back_x_ref, weight_ref, out_ref, spectrum_ref):
    spectrum = x_modes(received_ref[...], along_x_ref[...]).astype(BF)
    spectrum_ref[...] = spectrum
    lane = lax.broadcasted_iota(jnp.int32, (OWN * M, XC), 1)
    row = lax.broadcasted_iota(jnp.int32, (OWN * M, XC), 0) % M
    wide = spectrum.astype(F32)
    spread = jnp.concatenate(
        [jnp.where(lane // C + 2 * k == row, wide, 0.0).astype(BF) for k in range(M // 2)], axis=1
    )
    mixed = jnp.concatenate(
        [
            jnp.dot(spread[M * p : M * (p + 1)], weight_ref[p], preferred_element_type=F32)
            for p in range(OWN)
        ],
        axis=0,
    )
    twice = jnp.concatenate([mixed, mixed], axis=1)
    out_ref[...] = from_x_modes(twice, back_x_ref[...]).astype(out_ref.dtype)


def mix_back_kernel(received_ref, along_x_ref, back_x_ref, weight_ref, spectrum_ref, out_ref, both_ref):
    hat = x_modes(received_ref[...], along_x_ref[...]).astype(BF)
    lane = lax.broadcasted_iota(jnp.int32, (OWN * M, XC), 1)
    both_ref[...] = jnp.where(lane < C, spectrum_ref[...].astype(F32), hat.astype(F32)).astype(BF)
    lane = lax.broadcasted_iota(jnp.int32, (M, XC), 1)
    row = lax.broadcasted_iota(jnp.int32, (M, XC), 0)
    parts = []
    for p in range(OWN):
        every = lax.dot_general(
            hat[M * p : M * (p + 1), :C], weight_ref[p], (((1,), (1,)), ((), ())), preferred_element_type=F32
        )
        total = sum(
            jnp.where(lane // C + 2 * k == row, every[:, XC * k : XC * (k + 1)], 0.0) for k in range(M // 2)
        )
        parts.append(total + pltpu.roll(total, C, 1))
    out_ref[...] = from_x_modes(jnp.concatenate(parts, axis=0), back_x_ref[...]).astype(out_ref.dtype)


SMALL = pl.BlockSpec(memory_space=pltpu.VMEM)
LARGE = pl.BlockSpec(memory_space=pltpu.HBM)


def params(mib):
    return pltpu.CompilerParams(vmem_limit_bytes=mib * 1024 * 1024)


def cost(flops, size):
    return pl.CostEstimate(flops=flops, bytes_accessed=size, transcendentals=0)


ALL_BYTES = XC * N * N * 2
LARGE_OUT = pltpu.HBM((XC, N, N), BF)
PLANE_OUT = pltpu.HBM((C, N, N), BF)
MODES_OUT = pltpu.HBM((PAIRS, XC), BF)
MODES = pltpu.VMEM((PAIRS, XC), BF)
SMALL_OUT = jax.ShapeDtypeStruct((PAIRS, XC), BF)
OWN_OUT = jax.ShapeDtypeStruct((OWN * M, XC), BF)
WHOLE = pltpu.VMEM((XC, N, N), BF)
PLANE = pltpu.VMEM((C, N, N), BF)
SPREAD = pltpu.VMEM((XC * M, N), F32)


def large(array):
    return pltpu.with_memory_space_constraint(array, pltpu.HBM)


def sems(arrays, count):
    return pltpu.SemaphoreType.DMA((arrays, count))


def to_modes(field, table):
    small = (table["forward_y"], table["forward_z"])
    return pl.pallas_call(
        to_modes_kernel,
        in_specs=[LARGE] * 3,
        out_specs=LARGE,
        out_shape=MODES_OUT,
        scratch_shapes=[
            WHOLE, SPREAD, MODES, *[pltpu.VMEM(each.shape, BF) for each in small],
            pltpu.SemaphoreType.DMA((len(FIELD_CUTS) - 1,)), pltpu.SemaphoreType.DMA((3,)),
        ],
        compiler_params=params(40),
        cost_estimate=cost(XC * N * N * 128, ALL_BYTES),
        name="to_modes",
    )(large(field), *map(large, small))


def slopes(spatial, heads, points, cot, table):
    return pl.pallas_call(
        slope_kernel,
        in_specs=[SMALL] * 6 + [LARGE] * 3,
        out_specs=(LARGE, LARGE),
        out_shape=(LARGE_OUT, MODES_OUT),
        scratch_shapes=[SPREAD] * 2 + [MODES] + [WHOLE] * 3
        + [sems(4, len(SLOPE_OUT_CUTS)), pltpu.SemaphoreType.DMA],
        compiler_params=params(40),
        cost_estimate=cost(XC * N * N * 256, 3 * ALL_BYTES),
        name="slopes",
    )(
        spatial, table["forward_z"], table["back_y"], table["forward_y_half"], *heads,
        *map(large, points), large(cot),
    )


def result(back, wide, samples, head, point0, slope, table):
    return pl.pallas_call(
        result_kernel,
        in_specs=[SMALL] * 9 + [LARGE] * 2,
        out_specs=(LARGE, LARGE),
        out_shape=(LARGE_OUT, pltpu.HBM((OWN, M // 4, C, C), F32)),
        scratch_shapes=[
            SPREAD, WHOLE, PLANE, WHOLE, pltpu.VMEM((4, OWN * M, XC), F32), pltpu.VMEM((OWN, M // 4, C, C), F32),
            sems(2, len(RESULT_CUTS)), pltpu.SemaphoreType.DMA((STEPS,)), pltpu.SemaphoreType.DMA,
        ],
        compiler_params=params(40),
        cost_estimate=cost(XC * N * N * 512, 2 * ALL_BYTES),
        name="result",
    )(
        back, table["forward_z"], table["back_y"], wide, *samples, head, large(point0), large(slope)
    )


def pointwise(plane, back, weight, bias, array, table, cot=None):
    operands = [weight, table["spread"]] + ([] if back else [bias.reshape(1, C)])
    sources = ([] if cot is None else [cot]) + [array]
    wide = pltpu.VMEM((WIDE, WIDE), BF)
    head = pltpu.VMEM((RESULT_HEAD if back else SLOPE_HEAD, N, N), BF)
    kept = [head] * (0 if plane else 1 + (cot is not None)) + [wide] * back
    return pl.pallas_call(
        functools.partial(point_kernel, plane, back),
        in_specs=[SMALL] * len(operands) + [LARGE] * len(sources),
        out_specs=[LARGE] + [SMALL] * len(kept),
        out_shape=[PLANE_OUT] + kept,
        scratch_shapes=[wide] * (not back)
        + [PLANE, PLANE, pltpu.VMEM((WIDE, N), F32), sems(2, STEPS), pltpu.SemaphoreType.DMA],
        compiler_params=params(40),
        cost_estimate=cost(C * N * N * 1024, ALL_BYTES),
        name="pointwise",
    )(*operands, *map(large, sources))


def mix(received, weight, table):
    return pl.pallas_call(
        mix_kernel,
        in_specs=[SMALL] * 4,
        out_specs=(SMALL, SMALL),
        out_shape=(SMALL_OUT, OWN_OUT),
        compiler_params=params(40),
        cost_estimate=cost(1 << 27, 1 << 21),
        name="mix",
    )(received, table["along_x"], table["back_x"], weight)


def mix_back(received, weight, spectrum, table):
    return pl.pallas_call(
        mix_back_kernel,
        in_specs=[SMALL] * 5,
        out_specs=(SMALL, SMALL),
        out_shape=(SMALL_OUT, OWN_OUT),
        compiler_params=params(40),
        cost_estimate=cost(1 << 27, 1 << 21),
        name="mix_back",
    )(received, table["along_x"], table["back_x"], weight, spectrum)


def exchange(array):
    cut = array.reshape(GROUPS, OWN, XC)
    return lax.all_to_all(cut, "space", split_axis=0, concat_axis=0, tiled=True).reshape(PAIRS, XC)


def over_samples(both):
    def swap(array, k):
        return lax.ppermute(array, "dp", [(i, i ^ k) for i in range(4)])

    far = swap(both, 2)
    return [both, far, swap(both, 1), swap(far, 1)]


def per_device(field, cotangent, mode_weight, point_weight, point_bias):
    table = {name: jnp.asarray(value) for name, value in tables().items()}
    sample = field.reshape(XC, N, N)
    cot = cotangent.reshape(XC, N, N)
    weight = mode_weight.reshape(OWN, M * C, C)

    modes, sample = lax.optimization_barrier((to_modes(sample, table), sample))
    received = exchange(modes)
    point0, *heads = pointwise(0, False, point_weight, point_bias, sample, table, cot)
    received, point0 = lax.optimization_barrier((received, point0))
    spatial, spectrum = mix(received, weight, table)
    later, spatial = lax.optimization_barrier((sample, spatial))
    received = exchange(spatial)
    (point1,) = pointwise(1, False, point_weight, point_bias, later, table)
    slope, grad_modes = slopes(received, heads, (point0, point1), cot, table)
    received = exchange(grad_modes)
    point_back0, head, wide = pointwise(0, True, point_weight, None, slope, table)
    received, point_back0 = lax.optimization_barrier((received, point_back0))
    back, both = mix_back(received, weight, spectrum, table)
    field_grad, mode_grad = result(
        exchange(back), wide, over_samples(both), head, point_back0, slope, table
    )
    return field_grad.reshape(1, XL, C, N, N), mode_grad


def solution(mesh):
    return jax.shard_map(
        per_device,
        mesh=mesh,
        in_specs=(
            P("dp", "space", None, None, None),
            P("dp", "space", None, None, None),
            P("space", None, None, None),
            P(),
            P(),
        ),
        out_specs=(P("dp", "space", None, None, None), P("space", "dp", None, None)),
        check_vma=False,
    )
```

```python
import functools
import math

import jax
import jax.numpy as jnp
import numpy as np
from jax import lax
from jax.experimental import pallas as pl
from jax.experimental.pallas import tpu as pltpu
from jax.sharding import PartitionSpec as P

BF = jnp.bfloat16
F32 = jnp.float32

C = 64
M = 16
N = 128
XL = 2
XC = XL * C
PAIRS = M * M
OWN = 4
GROUPS = 64
SLOPE_HEAD = 16
RESULT_HEAD = 32


def basis(length, count):
    points = np.arange(length)[:, None]
    order = np.arange(count)[None, :]
    freq = (order + 1) // 2
    phase = (points * freq % length).astype(np.float32) * np.float32(2.0 * math.pi / length)
    cosine = np.logical_or(order % 2 == 1, order == 0)
    table = np.where(cosine, np.cos(phase), np.sin(phase)) * np.float32(math.sqrt(2.0 / length))
    return table.astype(np.float32)


def split(table):
    high = table.astype(BF)
    return high, (table - high.astype(np.float32)).astype(BF)


def tables():
    base = basis(N, M)
    table_z = base.astype(BF)
    forward_y = np.concatenate([np.kron(np.eye(2, dtype=np.float32), part.astype(np.float32).T) for part in split(base)])
    back_y = np.concatenate(split(base), axis=1)
    by_plane = base.reshape(GROUPS, XL, M)
    along_x = np.einsum("sxm,pq->xpmsq", by_plane, np.eye(OWN, dtype=np.float32)).reshape(XL * OWN * M, GROUPS * OWN)
    return dict(
        forward_y=forward_y.astype(BF),
        forward_y_half=(0.5 * forward_y).astype(BF),
        spread=np.kron(np.eye(C, dtype=np.float32), np.ones((ROWS, 1), np.float32)).astype(BF),
        back_y=back_y.astype(BF),
        forward_z=np.ascontiguousarray(table_z.T),
        along_x=np.stack(split(along_x)),
        back_x=np.stack(split(np.ascontiguousarray(along_x.T))),
    )


def y_modes(group, forward_y, scratch, row):
    block = jnp.concatenate(
        [jnp.concatenate(group[0:2], axis=0), jnp.concatenate(group[2:4], axis=0)], axis=1
    )
    both = jnp.dot(forward_y, block, preferred_element_type=F32)
    modes = both[: 2 * M] + both[2 * M :]
    scratch[pl.ds(row, 2 * M), :] = modes[:, :N]
    scratch[pl.ds(row + 2 * M, 2 * M), :] = modes[:, N:]


def z_modes(scratch, forward_z, modes, out_ref, sem):
    for a in range(M):
        part = scratch[pl.ds(a, XC, stride=M), :].astype(BF)
        modes[M * a : M * (a + 1), :] = lax.dot_general(
            forward_z, part, (((1,), (1,)), ((), ())), preferred_element_type=F32
        ).astype(BF)
    copy = pltpu.make_async_copy(modes, out_ref, sem)
    copy.start()
    return copy


def from_z_modes(modes, table_z, scratch):
    for a in range(M):
        scratch[pl.ds(a, XC, stride=M), :] = lax.dot_general(
            modes[M * a : M * (a + 1)], table_z, (((0,), (0,)), ((), ())), preferred_element_type=F32
        )


def from_y_modes(scratch, back_y, row):
    pair = jnp.concatenate(
        [scratch[pl.ds(row, M), :].astype(BF), scratch[pl.ds(row + M, M), :].astype(BF)], axis=1
    )
    return jnp.dot(back_y, jnp.concatenate([pair, pair], axis=0), preferred_element_type=F32)


def pieces(source, target, sems, cuts, first=0):
    return {
        low: pltpu.make_async_copy(
            source.at[pl.ds(low - first, high - low)], target.at[pl.ds(low, high - low)], sems.at[k]
        )
        for k, (low, high) in enumerate(zip(cuts, cuts[1:]))
    }


FIELD_CUTS = (0, 48, 96, 128)


def to_modes_kernel(
    field_ref, forward_y_ref, forward_z_ref, out_ref, held, scratch, modes, forward_y, forward_z, sems, small_sems
):
    small = [
        pltpu.make_async_copy(forward_y_ref, forward_y, small_sems.at[0]),
        pltpu.make_async_copy(forward_z_ref, forward_z, small_sems.at[1]),
    ]
    copies = pieces(field_ref, held, sems, FIELD_CUTS)
    for copy in (*small, *copies.values()):
        copy.start()
    for copy in small:
        copy.wait()
    for g in range(0, XC, 4):
        if g in copies:
            copies[g].wait()
        y_modes([held[g + j] for j in range(4)], forward_y[...], scratch, g * M)
    z_modes(scratch, forward_z[...], modes, out_ref, small_sems.at[2]).wait()


SLOPE_CUTS = (0, SLOPE_HEAD, 40, C, 96, 128)
SLOPE_OUT_CUTS = (0, 32, 64, 88, 104, 116, 128)
RESULT_CUTS = (0, RESULT_HEAD, C, C + RESULT_HEAD, 112, 128)
AHEAD = 2
BEHIND = 2


def ahead_of(product, count):
    ready = {}

    def take(at):
        for each in range(at, min(at + 2 * count + 2, XC), 2):
            if each not in ready:
                ready[each] = product(each)
        return ready[at]

    return take


def doubled_slope(pre, cot):
    root = math.sqrt(2.0 / math.pi)
    square = pre * pre
    tanh = jnp.tanh(pre * (root + (root * 0.044715) * square))
    outer = pre * (root + (root * 3 * 0.044715) * square)
    return (1.0 + tanh) * (1.0 + outer * (1.0 - tanh)) * cot


def slope_kernel(
    spatial_ref, table_z_ref, back_y_ref, forward_y_ref, point_head_ref, cot_head_ref,
    point0_ref, point1_ref, cot_ref, slope_ref, out_ref, spread, scratch, modes, point, cot, slope, sems, out_sem,
):
    point_copies = pieces(point0_ref, point, sems.at[0], SLOPE_CUTS[1:4])
    point_copies |= pieces(point1_ref, point, sems.at[1], SLOPE_CUTS[3:], C)
    cot_copies = pieces(cot_ref, cot, sems.at[2], SLOPE_CUTS[1:])
    slope_copies = pieces(slope, slope_ref, sems.at[3], SLOPE_OUT_CUTS)
    for low in SLOPE_CUTS[1:-1]:
        point_copies[low].start()
        cot_copies[low].start()
    from_z_modes(spatial_ref[...], table_z_ref[...], spread)
    spectral = ahead_of(lambda at: from_y_modes(spread, back_y_ref[...], at * M).astype(BF), AHEAD)
    waiting = []
    for first in range(0, XC, 4):
        if first in cot_copies:
            point_copies[first].wait()
            cot_copies[first].wait()
        point_at, cot_at = (point, cot) if first >= SLOPE_HEAD else (point_head_ref, cot_head_ref)
        group = []
        for at in range(first, first + 4, 2):
            both = spectral(at)
            for h in range(2):
                value = doubled_slope(both[:, N * h : N * (h + 1)] + point_at[at + h], cot_at[at + h])
                slope[at + h] = value
                group.append(value)
        waiting.append((group, first))
        if len(waiting) > BEHIND:
            group, row = waiting.pop(0)
            y_modes(group, forward_y_ref[...], scratch, row * M)
        for low, high in zip(SLOPE_OUT_CUTS, SLOPE_OUT_CUTS[1:]):
            if first + 4 == high:
                slope_copies[low].start()
    for group, row in waiting:
        y_modes(group, forward_y_ref[...], scratch, row * M)
    out_copy = z_modes(scratch, table_z_ref[...], modes, out_ref, out_sem)
    for copy in (*slope_copies.values(), out_copy):
        copy.wait()


def result_kernel(
    back_ref, table_z_ref, back_y_ref, both0_ref, both1_ref, both2_ref, both3_ref, head0_ref, head1_ref,
    point0_ref, point1_ref, out_ref, mode_grad_ref, spread, point, held, grads, total, sems, sem,
):
    head = head0_ref.shape[0]
    point_copies = pieces(point0_ref, point, sems.at[0], (head, C))
    point_copies |= pieces(point1_ref, point, sems.at[1], (C + head, XC), C)
    out_copies = pieces(held, out_ref, sems.at[2], RESULT_CUTS)
    for copy in point_copies.values():
        copy.start()
    mode_gradient((both0_ref, both1_ref, both2_ref, both3_ref), grads, total)
    mode_copy = pltpu.make_async_copy(total, mode_grad_ref, sem)
    mode_copy.start()
    from_z_modes(back_ref[...], table_z_ref[...], spread)
    spectral = ahead_of(lambda at: from_y_modes(spread, back_y_ref[...], at * M), 1)
    for low, high in zip(RESULT_CUTS, RESULT_CUTS[1:]):
        if low in point_copies:
            point_copies[low].wait()
        for g in range(low, high, 2):
            both = spectral(g)
            for h in range(2):
                plane, channel = divmod(g + h, C)
                other = (head0_ref, head1_ref)[plane][channel] if channel < head else point[g + h]
                held[g + h] = (both[:, N * h : N * (h + 1)] + other.astype(F32)).astype(BF)
        out_copies[low].start()
    for copy in (*out_copies.values(), mode_copy):
        copy.wait()


def mode_gradient(samples, grads, out_ref):
    quarter = M // len(samples)
    own = lax.axis_index("dp") * quarter
    for s, ref in enumerate(samples):
        grads[s] = ref[...].astype(F32)
    lane = lax.broadcasted_iota(jnp.int32, (M, quarter * C), 1)
    row = lax.broadcasted_iota(jnp.int32, (M, quarter * C), 0)
    for p in range(OWN):
        rows = jnp.concatenate([grads[s, pl.ds(p * M + own, quarter), :] for s in range(len(samples))], axis=0)
        spectrum = jnp.concatenate([rows[:, :C]] * quarter, axis=1)
        spectrum = jnp.where(lane // C == row % quarter, spectrum, 0.0).astype(BF)
        out_ref[p] = lax.dot_general(
            spectrum, rows[:, C:].astype(BF), (((0,), (0,)), ((), ())), preferred_element_type=F32
        ).reshape(quarter, C, C)


ROWS = 8
WIDE = C * ROWS


def widen(weight_ref, spread_ref, wide, transposed, factor):
    rows = lax.dot_general(
        spread_ref[...], weight_ref[...], (((1,), (int(transposed),)), ((), ())), preferred_element_type=F32
    ).astype(BF)
    for k in range(0, WIDE, 128):
        every = lax.dot_general(
            rows[k : k + 128], spread_ref[...], (((1,), (1,)), ((), ())), preferred_element_type=F32
        )
        row = lax.broadcasted_iota(jnp.int32, (128, WIDE), 0)
        column = lax.broadcasted_iota(jnp.int32, (128, WIDE), 1)
        wide[k : k + 128, :] = jnp.where(row % ROWS == column % ROWS, every * factor, 0.0).astype(BF)


YB = 32
STEPS = N // YB


def fetch_rows(source, target, sems, count=YB):
    def copy(k):
        at = (slice(None), pl.ds(k * count, count))
        return pltpu.make_async_copy(source.at[at], target.at[at], sems.at[k])

    return copy


def point_rows(array, wide, bias, out, k, count=YB):
    size = 256
    for y in range(k * count, (k + 1) * count, 2 * ROWS):
        values = array[:, y : y + 2 * ROWS, :].astype(F32)
        block = jnp.concatenate(
            [values[:, ROWS * h : ROWS * (h + 1)].reshape(WIDE, N).astype(BF) for h in range(2)], axis=1
        )
        for at in range(0, WIDE, size):
            part = jnp.dot(wide[at : at + size, :], block, preferred_element_type=F32)
            pieces = []
            for h in range(2):
                piece = part[:, N * h : N * (h + 1)]
                if bias is not None:
                    piece = piece + bias[at : at + size, :]
                pieces.append(piece.reshape(size // ROWS, ROWS, N))
            out[at // ROWS : (at + size) // ROWS, y : y + 2 * ROWS, :] = jnp.concatenate(pieces, axis=1).astype(
                out.dtype
            )


def point_kernel(plane, weight_ref, spread_ref, bias_ref, *refs):
    refs, (array, out, bias, wide, sems, head_sem) = refs[:-6], refs[-6:]
    if plane:
        in_ref, out_ref = refs
    else:
        cot_ref, in_ref, out_ref, head_ref, cot_head_ref = refs
        head_copy = pltpu.make_async_copy(cot_ref.at[pl.ds(0, SLOPE_HEAD)], cot_head_ref, head_sem)
    copy = fetch_rows(in_ref.at[pl.ds(plane * C, C)], array, sems.at[0])
    out_copy = fetch_rows(out, out_ref, sems.at[1])
    for k in range(STEPS):
        copy(k).start()
    if not plane:
        head_copy.start()
    bias[...] = lax.dot_general(
        spread_ref[...].astype(F32), jnp.broadcast_to(bias_ref[...], (N, C)), (((1,), (1,)), ((), ())),
        precision=lax.Precision.HIGHEST, preferred_element_type=F32,
    )
    widen(weight_ref, spread_ref, wide, True, 1.0)
    for k in range(STEPS):
        copy(k).wait()
        point_rows(array, wide, bias, out, k)
        out_copy(k).start()
    if not plane:
        head_ref[...] = out[:SLOPE_HEAD]
        head_copy.wait()
    for k in range(STEPS):
        out_copy(k).wait()


def point_back_kernel(plane, *refs):
    refs, (array, out, sems) = refs[:-3], refs[-3:]
    if plane:
        wide, in_ref, out_ref, head_ref = refs
    else:
        weight_ref, spread_ref, in_ref, out_ref, head_ref, wide = refs
    copy = fetch_rows(in_ref.at[pl.ds(plane * C, C)], array, sems.at[0])
    out_copy = fetch_rows(out, out_ref, sems.at[1])
    for k in range(STEPS):
        copy(k).start()
    if not plane:
        widen(weight_ref, spread_ref, wide, False, 0.5)
    for k in range(STEPS):
        copy(k).wait()
        point_rows(array, wide, None, out, k)
        out_copy(k).start()
    head_ref[...] = out[:RESULT_HEAD]
    for k in range(STEPS):
        out_copy(k).wait()


def x_modes(received, along_x):
    both = jnp.dot(along_x[0], received, preferred_element_type=F32)
    both += jnp.dot(along_x[1], received, preferred_element_type=F32)
    half = OWN * M
    lane = lax.broadcasted_iota(jnp.int32, (half, XC), 1)
    picked = jnp.where(lane < C, both[:half], both[half:])
    return picked + pltpu.roll(picked, C, 1)


def from_x_modes(twice, back_x):
    lane = lax.broadcasted_iota(jnp.int32, (OWN * M, XC), 1)
    stacked = jnp.concatenate([jnp.where(lane < C, twice, 0.0), jnp.where(lane < C, 0.0, twice)], axis=0)
    stacked = stacked.astype(BF)
    return jnp.dot(back_x[0], stacked, preferred_element_type=F32) + jnp.dot(
        back_x[1], stacked, preferred_element_type=F32
    )


def mix_kernel(received_ref, along_x_ref, back_x_ref, weight_ref, out_ref, spectrum_ref):
    spectrum = x_modes(received_ref[...], along_x_ref[...]).astype(BF)
    spectrum_ref[...] = spectrum
    lane = lax.broadcasted_iota(jnp.int32, (OWN * M, XC), 1)
    row = lax.broadcasted_iota(jnp.int32, (OWN * M, XC), 0) % M
    wide = spectrum.astype(F32)
    spread = jnp.concatenate(
        [jnp.where(lane // C + 2 * k == row, wide, 0.0).astype(BF) for k in range(M // 2)], axis=1
    )
    mixed = jnp.concatenate(
        [
            jnp.dot(spread[M * p : M * (p + 1)], weight_ref[p], preferred_element_type=F32)
            for p in range(OWN)
        ],
        axis=0,
    )
    twice = jnp.concatenate([mixed, mixed], axis=1)
    out_ref[...] = from_x_modes(twice, back_x_ref[...]).astype(out_ref.dtype)


def mix_back_kernel(received_ref, along_x_ref, back_x_ref, weight_ref, spectrum_ref, out_ref, both_ref):
    hat = x_modes(received_ref[...], along_x_ref[...]).astype(BF)
    lane = lax.broadcasted_iota(jnp.int32, (OWN * M, XC), 1)
    both_ref[...] = jnp.where(lane < C, spectrum_ref[...].astype(F32), hat.astype(F32)).astype(BF)
    lane = lax.broadcasted_iota(jnp.int32, (M, XC), 1)
    row = lax.broadcasted_iota(jnp.int32, (M, XC), 0)
    parts = []
    for p in range(OWN):
        every = lax.dot_general(
            hat[M * p : M * (p + 1), :C], weight_ref[p], (((1,), (1,)), ((), ())), preferred_element_type=F32
        )
        total = sum(
            jnp.where(lane // C + 2 * k == row, every[:, XC * k : XC * (k + 1)], 0.0) for k in range(M // 2)
        )
        parts.append(total + pltpu.roll(total, C, 1))
    out_ref[...] = from_x_modes(jnp.concatenate(parts, axis=0), back_x_ref[...]).astype(out_ref.dtype)


SMALL = pl.BlockSpec(memory_space=pltpu.VMEM)
LARGE = pl.BlockSpec(memory_space=pltpu.HBM)


def params(mib):
    return pltpu.CompilerParams(vmem_limit_bytes=mib * 1024 * 1024)


def cost(flops, size):
    return pl.CostEstimate(flops=flops, bytes_accessed=size, transcendentals=0)


ALL_BYTES = XC * N * N * 2
LARGE_OUT = pltpu.HBM((XC, N, N), BF)
PLANE_OUT = pltpu.HBM((C, N, N), BF)
MODES_OUT = pltpu.HBM((PAIRS, XC), BF)
MODES = pltpu.VMEM((PAIRS, XC), BF)
SMALL_OUT = jax.ShapeDtypeStruct((PAIRS, XC), BF)
OWN_OUT = jax.ShapeDtypeStruct((OWN * M, XC), BF)
WHOLE = pltpu.VMEM((XC, N, N), BF)
PLANE = pltpu.VMEM((C, N, N), BF)
SPREAD = pltpu.VMEM((XC * M, N), F32)


def large(array):
    return pltpu.with_memory_space_constraint(array, pltpu.HBM)


def sems(arrays, count):
    return pltpu.SemaphoreType.DMA((arrays, count))


def to_modes(field, table):
    small = (table["forward_y"], table["forward_z"])
    return pl.pallas_call(
        to_modes_kernel,
        in_specs=[LARGE] * 3,
        out_specs=LARGE,
        out_shape=MODES_OUT,
        scratch_shapes=[
            WHOLE, SPREAD, MODES, *[pltpu.VMEM(each.shape, BF) for each in small],
            pltpu.SemaphoreType.DMA((len(FIELD_CUTS) - 1,)), pltpu.SemaphoreType.DMA((3,)),
        ],
        compiler_params=params(40),
        cost_estimate=cost(XC * N * N * 128, ALL_BYTES),
        name="to_modes",
    )(large(field), *map(large, small))


def slopes(spatial, heads, points, cot, table):
    return pl.pallas_call(
        slope_kernel,
        in_specs=[SMALL] * 6 + [LARGE] * 3,
        out_specs=(LARGE, LARGE),
        out_shape=(LARGE_OUT, MODES_OUT),
        scratch_shapes=[SPREAD] * 2 + [MODES] + [WHOLE] * 3
        + [sems(4, len(SLOPE_OUT_CUTS)), pltpu.SemaphoreType.DMA],
        compiler_params=params(40),
        cost_estimate=cost(XC * N * N * 256, 3 * ALL_BYTES),
        name="slopes",
    )(
        spatial, table["forward_z"], table["back_y"], table["forward_y_half"], *heads,
        *map(large, points), large(cot),
    )


def result(back, samples, heads, points, table):
    return pl.pallas_call(
        result_kernel,
        in_specs=[SMALL] * 9 + [LARGE] * 2,
        out_specs=(LARGE, LARGE),
        out_shape=(LARGE_OUT, pltpu.HBM((OWN, M // 4, C, C), F32)),
        scratch_shapes=[
            SPREAD, WHOLE, WHOLE, pltpu.VMEM((4, OWN * M, XC), F32), pltpu.VMEM((OWN, M // 4, C, C), F32),
            sems(3, len(RESULT_CUTS)), pltpu.SemaphoreType.DMA,
        ],
        compiler_params=params(40),
        cost_estimate=cost(XC * N * N * 128, 2 * ALL_BYTES),
        name="result",
    )(back, table["forward_z"], table["back_y"], *samples, *heads, *map(large, points))


WIDENED = pltpu.VMEM((WIDE, WIDE), BF)
HALF = dict(
    compiler_params=params(40), cost_estimate=cost(C * N * N * 1024, ALL_BYTES), name="pointwise"
)


def pointwise(plane, weight, bias, array, table, cot=None):
    sources = ([] if cot is None else [cot]) + [array]
    heads = [pltpu.VMEM((SLOPE_HEAD, N, N), BF)] * (0 if plane else 2)
    return pl.pallas_call(
        functools.partial(point_kernel, plane),
        in_specs=[SMALL] * 3 + [LARGE] * len(sources),
        out_specs=[LARGE] + [SMALL] * len(heads),
        out_shape=[PLANE_OUT] + heads,
        scratch_shapes=[PLANE, PLANE, pltpu.VMEM((WIDE, N), F32), WIDENED, sems(2, STEPS), pltpu.SemaphoreType.DMA],
        **HALF,
    )(weight, table["spread"], bias.reshape(1, C), *map(large, sources))


def pointwise_back(plane, weights, array):
    kept = [pltpu.VMEM((RESULT_HEAD, N, N), BF)] + [WIDENED] * (not plane)
    return pl.pallas_call(
        functools.partial(point_back_kernel, plane),
        in_specs=[SMALL] * len(weights) + [LARGE],
        out_specs=[LARGE] + [SMALL] * len(kept),
        out_shape=[PLANE_OUT] + kept,
        scratch_shapes=[PLANE, PLANE, sems(2, STEPS)],
        **HALF,
    )(*weights, large(array))


def mix(received, weight, table):
    return pl.pallas_call(
        mix_kernel,
        in_specs=[SMALL] * 4,
        out_specs=(SMALL, SMALL),
        out_shape=(SMALL_OUT, OWN_OUT),
        compiler_params=params(40),
        cost_estimate=cost(1 << 27, 1 << 21),
        name="mix",
    )(received, table["along_x"], table["back_x"], weight)


def mix_back(received, weight, spectrum, table):
    return pl.pallas_call(
        mix_back_kernel,
        in_specs=[SMALL] * 5,
        out_specs=(SMALL, SMALL),
        out_shape=(SMALL_OUT, OWN_OUT),
        compiler_params=params(40),
        cost_estimate=cost(1 << 27, 1 << 21),
        name="mix_back",
    )(received, table["along_x"], table["back_x"], weight, spectrum)


def exchange(array):
    cut = array.reshape(GROUPS, OWN, XC)
    return lax.all_to_all(cut, "space", split_axis=0, concat_axis=0, tiled=True).reshape(PAIRS, XC)


def over_samples(both):
    return [both] + [lax.ppermute(both, "dp", [(i, i ^ k) for i in range(4)]) for k in (2, 3, 1)]


def per_device(field, cotangent, mode_weight, point_weight, point_bias):
    table = {name: jnp.asarray(value) for name, value in tables().items()}
    sample = field.reshape(XC, N, N)
    cot = cotangent.reshape(XC, N, N)
    weight = mode_weight.reshape(OWN, M * C, C)

    modes, sample = lax.optimization_barrier((to_modes(sample, table), sample))
    received = exchange(modes)
    point0, *heads = pointwise(0, point_weight, point_bias, sample, table, cot)
    received, point0 = lax.optimization_barrier((received, point0))
    spatial, spectrum = mix(received, weight, table)
    later, spatial = lax.optimization_barrier((sample, spatial))
    received = exchange(spatial)
    (point1,) = pointwise(1, point_weight, point_bias, later, table)
    slope, grad_modes = slopes(received, heads, (point0, point1), cot, table)
    received = exchange(grad_modes)
    point_back0, head0, wide = pointwise_back(0, (point_weight, table["spread"]), slope)
    received, point_back0 = lax.optimization_barrier((received, point_back0))
    back, both = mix_back(received, weight, spectrum, table)
    later, back = lax.optimization_barrier((slope, back))
    back = exchange(back)
    point_back1, head1 = pointwise_back(1, (wide,), later)
    field_grad, mode_grad = result(
        back, over_samples(both), (head0, head1), (point_back0, point_back1), table
    )
    return field_grad.reshape(1, XL, C, N, N), mode_grad


def solution(mesh):
    return jax.shard_map(
        per_device,
        mesh=mesh,
        in_specs=(
            P("dp", "space", None, None, None),
            P("dp", "space", None, None, None),
            P("space", None, None, None),
            P(),
            P(),
        ),
        out_specs=(P("dp", "space", None, None, None), P("space", "dp", None, None)),
        check_vma=False,
    )
```

```python
import functools
import math

import jax
import jax.numpy as jnp
import numpy as np
from jax import lax
from jax.experimental import pallas as pl
from jax.experimental.pallas import tpu as pltpu
from jax.sharding import PartitionSpec as P

BF = jnp.bfloat16
F32 = jnp.float32

C = 64
M = 16
N = 128
XL = 2
XC = XL * C
PAIRS = M * M
OWN = 4
GROUPS = 64
SLOPE_HEAD = 16
RESULT_HEADS = (32, 48)


def basis(length, count):
    points = np.arange(length)[:, None]
    order = np.arange(count)[None, :]
    freq = (order + 1) // 2
    phase = (points * freq % length).astype(np.float32) * np.float32(2.0 * math.pi / length)
    cosine = np.logical_or(order % 2 == 1, order == 0)
    table = np.where(cosine, np.cos(phase), np.sin(phase)) * np.float32(math.sqrt(2.0 / length))
    return table.astype(np.float32)


def split(table):
    high = table.astype(BF)
    return high, (table - high.astype(np.float32)).astype(BF)


def tables():
    base = basis(N, M)
    table_z = base.astype(BF)
    forward_y = np.concatenate([np.kron(np.eye(2, dtype=np.float32), part.astype(np.float32).T) for part in split(base)])
    back_y = np.concatenate(split(base), axis=1)
    by_plane = base.reshape(GROUPS, XL, M)
    along_x = np.einsum("sxm,pq->xpmsq", by_plane, np.eye(OWN, dtype=np.float32)).reshape(XL * OWN * M, GROUPS * OWN)
    return dict(
        forward_y=forward_y.astype(BF),
        forward_y_half=(0.5 * forward_y).astype(BF),
        spread=np.kron(np.eye(C, dtype=np.float32), np.ones((ROWS, 1), np.float32)).astype(BF),
        back_y=back_y.astype(BF),
        forward_z=np.ascontiguousarray(table_z.T),
        along_x=np.stack(split(along_x)),
        back_x=np.stack(split(np.ascontiguousarray(along_x.T))),
    )


def y_modes(group, forward_y, scratch, row):
    block = jnp.concatenate(
        [jnp.concatenate(group[0:2], axis=0), jnp.concatenate(group[2:4], axis=0)], axis=1
    )
    both = jnp.dot(forward_y, block, preferred_element_type=F32)
    modes = both[: 2 * M] + both[2 * M :]
    scratch[pl.ds(row, 2 * M), :] = modes[:, :N]
    scratch[pl.ds(row + 2 * M, 2 * M), :] = modes[:, N:]


def z_modes(scratch, forward_z, modes, out_ref, sem):
    for a in range(M):
        part = scratch[pl.ds(a, XC, stride=M), :].astype(BF)
        modes[M * a : M * (a + 1), :] = lax.dot_general(
            forward_z, part, (((1,), (1,)), ((), ())), preferred_element_type=F32
        ).astype(BF)
    copy = pltpu.make_async_copy(modes, out_ref, sem)
    copy.start()
    return copy


def from_z_modes(modes, table_z, scratch):
    for a in range(M):
        scratch[pl.ds(a, XC, stride=M), :] = lax.dot_general(
            modes[M * a : M * (a + 1)], table_z, (((0,), (0,)), ((), ())), preferred_element_type=F32
        )


def from_y_modes(scratch, back_y, row):
    pair = jnp.concatenate(
        [scratch[pl.ds(row, M), :].astype(BF), scratch[pl.ds(row + M, M), :].astype(BF)], axis=1
    )
    return jnp.dot(back_y, jnp.concatenate([pair, pair], axis=0), preferred_element_type=F32)


def pieces(source, target, sems, cuts, first=0):
    return {
        low: pltpu.make_async_copy(
            source.at[pl.ds(low - first, high - low)], target.at[pl.ds(low, high - low)], sems.at[k]
        )
        for k, (low, high) in enumerate(zip(cuts, cuts[1:]))
    }


FIELD_CUTS = (0, 48, 96, 128)


def to_modes_kernel(
    field_ref, forward_y_ref, forward_z_ref, out_ref, held, scratch, modes, forward_y, forward_z, sems, small_sems
):
    small = [
        pltpu.make_async_copy(forward_y_ref, forward_y, small_sems.at[0]),
        pltpu.make_async_copy(forward_z_ref, forward_z, small_sems.at[1]),
    ]
    copies = pieces(field_ref, held, sems, FIELD_CUTS)
    for copy in (*small, *copies.values()):
        copy.start()
    for copy in small:
        copy.wait()
    for g in range(0, XC, 4):
        if g in copies:
            copies[g].wait()
        y_modes([held[g + j] for j in range(4)], forward_y[...], scratch, g * M)
    z_modes(scratch, forward_z[...], modes, out_ref, small_sems.at[2]).wait()


SLOPE_CUTS = (0, SLOPE_HEAD, 40, C, 96, 128)
SLOPE_OUT_CUTS = (0, 32, 64, 88, 104, 116, 128)
RESULT_CUTS = (0, RESULT_HEADS[0], C, 96, C + RESULT_HEADS[1], 128)
AHEAD = 2
BEHIND = 2


def ahead_of(product, count):
    ready = {}

    def take(at):
        for each in range(at, min(at + 2 * count + 2, XC), 2):
            if each not in ready:
                ready[each] = product(each)
        return ready[at]

    return take


def doubled_slope(pre, cot):
    root = math.sqrt(2.0 / math.pi)
    square = pre * pre
    tanh = jnp.tanh(pre * (root + (root * 0.044715) * square))
    outer = pre * (root + (root * 3 * 0.044715) * square)
    return (1.0 + tanh) * (1.0 + outer * (1.0 - tanh)) * cot


def slope_kernel(
    spatial_ref, table_z_ref, back_y_ref, forward_y_ref, point_head_ref, cot_head_ref,
    point0_ref, point1_ref, cot_ref, slope_ref, out_ref, spread, scratch, modes, point, cot, slope, sems, out_sem,
):
    point_copies = pieces(point0_ref, point, sems.at[0], SLOPE_CUTS[1:4])
    point_copies |= pieces(point1_ref, point, sems.at[1], SLOPE_CUTS[3:], C)
    cot_copies = pieces(cot_ref, cot, sems.at[2], SLOPE_CUTS[1:])
    slope_copies = pieces(slope, slope_ref, sems.at[3], SLOPE_OUT_CUTS)
    for low in SLOPE_CUTS[1:-1]:
        point_copies[low].start()
        cot_copies[low].start()
    from_z_modes(spatial_ref[...], table_z_ref[...], spread)
    spectral = ahead_of(lambda at: from_y_modes(spread, back_y_ref[...], at * M).astype(BF), AHEAD)
    waiting = []
    for first in range(0, XC, 4):
        if first in cot_copies:
            point_copies[first].wait()
            cot_copies[first].wait()
        point_at, cot_at = (point, cot) if first >= SLOPE_HEAD else (point_head_ref, cot_head_ref)
        group = []
        for at in range(first, first + 4, 2):
            both = spectral(at)
            for h in range(2):
                value = doubled_slope(both[:, N * h : N * (h + 1)] + point_at[at + h], cot_at[at + h])
                slope[at + h] = value
                group.append(value)
        waiting.append((group, first))
        if len(waiting) > BEHIND:
            group, row = waiting.pop(0)
            y_modes(group, forward_y_ref[...], scratch, row * M)
        for low, high in zip(SLOPE_OUT_CUTS, SLOPE_OUT_CUTS[1:]):
            if first + 4 == high:
                slope_copies[low].start()
    for group, row in waiting:
        y_modes(group, forward_y_ref[...], scratch, row * M)
    out_copy = z_modes(scratch, table_z_ref[...], modes, out_ref, out_sem)
    for copy in (*slope_copies.values(), out_copy):
        copy.wait()


def result_kernel(
    back_ref, table_z_ref, back_y_ref, both0_ref, both1_ref, both2_ref, both3_ref, head0_ref, head1_ref,
    point0_ref, point1_ref, out_ref, mode_grad_ref, spread, point, held, grads, total, sems, sem,
):
    point_copies = pieces(point0_ref, point, sems.at[0], (RESULT_HEADS[0], C))
    point_copies |= pieces(point1_ref, point, sems.at[1], (C + RESULT_HEADS[1], XC), C)
    out_copies = pieces(held, out_ref, sems.at[2], RESULT_CUTS)
    for copy in point_copies.values():
        copy.start()
    mode_gradient((both0_ref, both1_ref, both2_ref, both3_ref), grads, total)
    mode_copy = pltpu.make_async_copy(total, mode_grad_ref, sem)
    mode_copy.start()
    from_z_modes(back_ref[...], table_z_ref[...], spread)
    spectral = ahead_of(lambda at: from_y_modes(spread, back_y_ref[...], at * M), 1)
    for low, high in zip(RESULT_CUTS, RESULT_CUTS[1:]):
        if low in point_copies:
            point_copies[low].wait()
        for g in range(low, high, 2):
            both = spectral(g)
            for h in range(2):
                plane, channel = divmod(g + h, C)
                head = (head0_ref, head1_ref)[plane]
                other = head[channel] if channel < RESULT_HEADS[plane] else point[g + h]
                held[g + h] = (both[:, N * h : N * (h + 1)] + other.astype(F32)).astype(BF)
        out_copies[low].start()
    for copy in (*out_copies.values(), mode_copy):
        copy.wait()


def mode_gradient(samples, grads, out_ref):
    quarter = M // len(samples)
    own = lax.axis_index("dp") * quarter
    for s, ref in enumerate(samples):
        grads[s] = ref[...].astype(F32)
    lane = lax.broadcasted_iota(jnp.int32, (M, quarter * C), 1)
    row = lax.broadcasted_iota(jnp.int32, (M, quarter * C), 0)
    for p in range(OWN):
        rows = jnp.concatenate([grads[s, pl.ds(p * M + own, quarter), :] for s in range(len(samples))], axis=0)
        spectrum = jnp.concatenate([rows[:, :C]] * quarter, axis=1)
        spectrum = jnp.where(lane // C == row % quarter, spectrum, 0.0).astype(BF)
        out_ref[p] = lax.dot_general(
            spectrum, rows[:, C:].astype(BF), (((0,), (0,)), ((), ())), preferred_element_type=F32
        ).reshape(quarter, C, C)


ROWS = 8
WIDE = C * ROWS


def widen(weight_ref, spread_ref, wide, transposed, factor):
    rows = lax.dot_general(
        spread_ref[...], weight_ref[...], (((1,), (int(transposed),)), ((), ())), preferred_element_type=F32
    ).astype(BF)
    for k in range(0, WIDE, 128):
        every = lax.dot_general(
            rows[k : k + 128], spread_ref[...], (((1,), (1,)), ((), ())), preferred_element_type=F32
        )
        row = lax.broadcasted_iota(jnp.int32, (128, WIDE), 0)
        column = lax.broadcasted_iota(jnp.int32, (128, WIDE), 1)
        wide[k : k + 128, :] = jnp.where(row % ROWS == column % ROWS, every * factor, 0.0).astype(BF)


YB = 32
STEPS = N // YB


def fetch_rows(source, target, sems, count=YB):
    def copy(k):
        at = (slice(None), pl.ds(k * count, count))
        return pltpu.make_async_copy(source.at[at], target.at[at], sems.at[k])

    return copy


def point_rows(array, wide, bias, out, k, count=YB):
    size = 256
    for y in range(k * count, (k + 1) * count, 2 * ROWS):
        values = array[:, y : y + 2 * ROWS, :].astype(F32)
        block = jnp.concatenate(
            [values[:, ROWS * h : ROWS * (h + 1)].reshape(WIDE, N).astype(BF) for h in range(2)], axis=1
        )
        for at in range(0, WIDE, size):
            part = jnp.dot(wide[at : at + size, :], block, preferred_element_type=F32)
            pieces = []
            for h in range(2):
                piece = part[:, N * h : N * (h + 1)]
                if bias is not None:
                    piece = piece + bias[at : at + size, :]
                pieces.append(piece.reshape(size // ROWS, ROWS, N))
            out[at // ROWS : (at + size) // ROWS, y : y + 2 * ROWS, :] = jnp.concatenate(pieces, axis=1).astype(
                out.dtype
            )


def point_kernel(plane, weight_ref, spread_ref, bias_ref, *refs):
    refs, (array, out, bias, wide, sems, head_sem) = refs[:-6], refs[-6:]
    if plane:
        in_ref, out_ref = refs
    else:
        cot_ref, in_ref, out_ref, head_ref, cot_head_ref = refs
        head_copy = pltpu.make_async_copy(cot_ref.at[pl.ds(0, SLOPE_HEAD)], cot_head_ref, head_sem)
    copy = fetch_rows(in_ref.at[pl.ds(plane * C, C)], array, sems.at[0])
    out_copy = fetch_rows(out, out_ref, sems.at[1])
    for k in range(STEPS):
        copy(k).start()
    if not plane:
        head_copy.start()
    high = bias_ref[...].astype(BF)
    low = (bias_ref[...] - high.astype(F32)).astype(BF)
    bias[...] = sum(
        lax.dot_general(
            spread_ref[...], jnp.broadcast_to(part, (N, C)), (((1,), (1,)), ((), ())), preferred_element_type=F32
        )
        for part in (high, low)
    )
    widen(weight_ref, spread_ref, wide, True, 1.0)
    for k in range(STEPS):
        copy(k).wait()
        point_rows(array, wide, bias, out, k)
        out_copy(k).start()
    if not plane:
        head_ref[...] = out[:SLOPE_HEAD]
        head_copy.wait()
    for k in range(STEPS):
        out_copy(k).wait()


def point_back_kernel(plane, *refs):
    refs, (array, out, sems) = refs[:-3], refs[-3:]
    if plane:
        wide, in_ref, out_ref, head_ref = refs
    else:
        weight_ref, spread_ref, in_ref, out_ref, head_ref, wide = refs
    copy = fetch_rows(in_ref.at[pl.ds(plane * C, C)], array, sems.at[0])
    out_copy = fetch_rows(out, out_ref, sems.at[1])
    for k in range(STEPS):
        copy(k).start()
    if not plane:
        widen(weight_ref, spread_ref, wide, False, 0.5)
    for k in range(STEPS):
        copy(k).wait()
        point_rows(array, wide, None, out, k)
        out_copy(k).start()
    head_ref[...] = out[: RESULT_HEADS[plane]]
    for k in range(STEPS):
        out_copy(k).wait()


def x_modes(received, along_x):
    both = jnp.dot(along_x[0], received, preferred_element_type=F32)
    both += jnp.dot(along_x[1], received, preferred_element_type=F32)
    half = OWN * M
    lane = lax.broadcasted_iota(jnp.int32, (half, XC), 1)
    picked = jnp.where(lane < C, both[:half], both[half:])
    return picked + pltpu.roll(picked, C, 1)


def from_x_modes(twice, back_x):
    lane = lax.broadcasted_iota(jnp.int32, (OWN * M, XC), 1)
    stacked = jnp.concatenate([jnp.where(lane < C, twice, 0.0), jnp.where(lane < C, 0.0, twice)], axis=0)
    stacked = stacked.astype(BF)
    return jnp.dot(back_x[0], stacked, preferred_element_type=F32) + jnp.dot(
        back_x[1], stacked, preferred_element_type=F32
    )


def mix_kernel(received_ref, along_x_ref, back_x_ref, weight_ref, out_ref, spectrum_ref):
    spectrum = x_modes(received_ref[...], along_x_ref[...]).astype(BF)
    spectrum_ref[...] = spectrum
    lane = lax.broadcasted_iota(jnp.int32, (OWN * M, XC), 1)
    row = lax.broadcasted_iota(jnp.int32, (OWN * M, XC), 0) % M
    wide = spectrum.astype(F32)
    spread = jnp.concatenate(
        [jnp.where(lane // C + 2 * k == row, wide, 0.0).astype(BF) for k in range(M // 2)], axis=1
    )
    mixed = jnp.concatenate(
        [
            jnp.dot(spread[M * p : M * (p + 1)], weight_ref[p], preferred_element_type=F32)
            for p in range(OWN)
        ],
        axis=0,
    )
    twice = jnp.concatenate([mixed, mixed], axis=1)
    out_ref[...] = from_x_modes(twice, back_x_ref[...]).astype(out_ref.dtype)


def mix_back_kernel(received_ref, along_x_ref, back_x_ref, weight_ref, spectrum_ref, out_ref, both_ref):
    hat = x_modes(received_ref[...], along_x_ref[...]).astype(BF)
    lane = lax.broadcasted_iota(jnp.int32, (OWN * M, XC), 1)
    both_ref[...] = jnp.where(lane < C, spectrum_ref[...].astype(F32), hat.astype(F32)).astype(BF)
    lane = lax.broadcasted_iota(jnp.int32, (M, XC), 1)
    row = lax.broadcasted_iota(jnp.int32, (M, XC), 0)
    parts = []
    for p in range(OWN):
        every = lax.dot_general(
            hat[M * p : M * (p + 1), :C], weight_ref[p], (((1,), (1,)), ((), ())), preferred_element_type=F32
        )
        total = sum(
            jnp.where(lane // C + 2 * k == row, every[:, XC * k : XC * (k + 1)], 0.0) for k in range(M // 2)
        )
        parts.append(total + pltpu.roll(total, C, 1))
    out_ref[...] = from_x_modes(jnp.concatenate(parts, axis=0), back_x_ref[...]).astype(out_ref.dtype)


SMALL = pl.BlockSpec(memory_space=pltpu.VMEM)
LARGE = pl.BlockSpec(memory_space=pltpu.HBM)


def params(mib):
    return pltpu.CompilerParams(vmem_limit_bytes=mib * 1024 * 1024)


def cost(flops, size):
    return pl.CostEstimate(flops=flops, bytes_accessed=size, transcendentals=0)


ALL_BYTES = XC * N * N * 2
LARGE_OUT = pltpu.HBM((XC, N, N), BF)
PLANE_OUT = pltpu.HBM((C, N, N), BF)
MODES_OUT = pltpu.HBM((PAIRS, XC), BF)
MODES = pltpu.VMEM((PAIRS, XC), BF)
SMALL_OUT = jax.ShapeDtypeStruct((PAIRS, XC), BF)
OWN_OUT = jax.ShapeDtypeStruct((OWN * M, XC), BF)
WHOLE = pltpu.VMEM((XC, N, N), BF)
PLANE = pltpu.VMEM((C, N, N), BF)
SPREAD = pltpu.VMEM((XC * M, N), F32)


def large(array):
    return pltpu.with_memory_space_constraint(array, pltpu.HBM)


def sems(arrays, count):
    return pltpu.SemaphoreType.DMA((arrays, count))


def to_modes(field, table):
    small = (table["forward_y"], table["forward_z"])
    return pl.pallas_call(
        to_modes_kernel,
        in_specs=[LARGE] * 3,
        out_specs=LARGE,
        out_shape=MODES_OUT,
        scratch_shapes=[
            WHOLE, SPREAD, MODES, *[pltpu.VMEM(each.shape, BF) for each in small],
            pltpu.SemaphoreType.DMA((len(FIELD_CUTS) - 1,)), pltpu.SemaphoreType.DMA((3,)),
        ],
        compiler_params=params(40),
        cost_estimate=cost(XC * N * N * 128, ALL_BYTES),
        name="to_modes",
    )(large(field), *map(large, small))


def slopes(spatial, heads, points, cot, table):
    return pl.pallas_call(
        slope_kernel,
        in_specs=[SMALL] * 6 + [LARGE] * 3,
        out_specs=(LARGE, LARGE),
        out_shape=(LARGE_OUT, MODES_OUT),
        scratch_shapes=[SPREAD] * 2 + [MODES] + [WHOLE] * 3
        + [sems(4, len(SLOPE_OUT_CUTS)), pltpu.SemaphoreType.DMA],
        compiler_params=params(40),
        cost_estimate=cost(XC * N * N * 256, 3 * ALL_BYTES),
        name="slopes",
    )(
        spatial, table["forward_z"], table["back_y"], table["forward_y_half"], *heads,
        *map(large, points), large(cot),
    )


def result(back, samples, heads, points, table):
    return pl.pallas_call(
        result_kernel,
        in_specs=[SMALL] * 9 + [LARGE] * 2,
        out_specs=(LARGE, LARGE),
        out_shape=(LARGE_OUT, pltpu.HBM((OWN, M // 4, C, C), F32)),
        scratch_shapes=[
            SPREAD, WHOLE, WHOLE, pltpu.VMEM((4, OWN * M, XC), F32), pltpu.VMEM((OWN, M // 4, C, C), F32),
            sems(3, len(RESULT_CUTS)), pltpu.SemaphoreType.DMA,
        ],
        compiler_params=params(40),
        cost_estimate=cost(XC * N * N * 128, 2 * ALL_BYTES),
        name="result",
    )(back, table["forward_z"], table["back_y"], *samples, *heads, *map(large, points))


WIDENED = pltpu.VMEM((WIDE, WIDE), BF)
HALF = dict(
    compiler_params=params(40), cost_estimate=cost(C * N * N * 1024, ALL_BYTES), name="pointwise"
)


def pointwise(plane, weight, bias, array, table, cot=None):
    sources = ([] if cot is None else [cot]) + [array]
    heads = [pltpu.VMEM((SLOPE_HEAD, N, N), BF)] * (0 if plane else 2)
    return pl.pallas_call(
        functools.partial(point_kernel, plane),
        in_specs=[SMALL] * 3 + [LARGE] * len(sources),
        out_specs=[LARGE] + [SMALL] * len(heads),
        out_shape=[PLANE_OUT] + heads,
        scratch_shapes=[PLANE, PLANE, pltpu.VMEM((WIDE, N), F32), WIDENED, sems(2, STEPS), pltpu.SemaphoreType.DMA],
        **HALF,
    )(weight, table["spread"], bias.reshape(1, C), *map(large, sources))


def pointwise_back(plane, weights, array):
    kept = [pltpu.VMEM((RESULT_HEADS[plane], N, N), BF)] + [WIDENED] * (not plane)
    return pl.pallas_call(
        functools.partial(point_back_kernel, plane),
        in_specs=[SMALL] * len(weights) + [LARGE],
        out_specs=[LARGE] + [SMALL] * len(kept),
        out_shape=[PLANE_OUT] + kept,
        scratch_shapes=[PLANE, PLANE, sems(2, STEPS)],
        **HALF,
    )(*weights, large(array))


def mix(received, weight, table):
    return pl.pallas_call(
        mix_kernel,
        in_specs=[SMALL] * 4,
        out_specs=(SMALL, SMALL),
        out_shape=(SMALL_OUT, OWN_OUT),
        compiler_params=params(40),
        cost_estimate=cost(1 << 27, 1 << 21),
        name="mix",
    )(received, table["along_x"], table["back_x"], weight)


def mix_back(received, weight, spectrum, table):
    return pl.pallas_call(
        mix_back_kernel,
        in_specs=[SMALL] * 5,
        out_specs=(SMALL, SMALL),
        out_shape=(SMALL_OUT, OWN_OUT),
        compiler_params=params(40),
        cost_estimate=cost(1 << 27, 1 << 21),
        name="mix_back",
    )(received, table["along_x"], table["back_x"], weight, spectrum)


def exchange(array):
    cut = array.reshape(GROUPS, OWN, XC)
    return lax.all_to_all(cut, "space", split_axis=0, concat_axis=0, tiled=True).reshape(PAIRS, XC)


def over_samples(both):
    return [both] + [lax.ppermute(both, "dp", [(i, i ^ k) for i in range(4)]) for k in (2, 3, 1)]


def per_device(field, cotangent, mode_weight, point_weight, point_bias):
    table = {name: jnp.asarray(value) for name, value in tables().items()}
    sample = field.reshape(XC, N, N)
    cot = cotangent.reshape(XC, N, N)
    weight = mode_weight.reshape(OWN, M * C, C)

    modes, sample = lax.optimization_barrier((to_modes(sample, table), sample))
    received = exchange(modes)
    point0, *heads = pointwise(0, point_weight, point_bias, sample, table, cot)
    received, point0 = lax.optimization_barrier((received, point0))
    spatial, spectrum = mix(received, weight, table)
    later, spatial = lax.optimization_barrier((sample, spatial))
    received = exchange(spatial)
    (point1,) = pointwise(1, point_weight, point_bias, later, table)
    slope, grad_modes = slopes(received, heads, (point0, point1), cot, table)
    received = exchange(grad_modes)
    point_back0, head0, wide = pointwise_back(0, (point_weight, table["spread"]), slope)
    received, point_back0 = lax.optimization_barrier((received, point_back0))
    back, both = mix_back(received, weight, spectrum, table)
    later, back = lax.optimization_barrier((slope, back))
    back = exchange(back)
    point_back1, head1 = pointwise_back(1, (wide,), later)
    field_grad, mode_grad = result(
        back, over_samples(both), (head0, head1), (point_back0, point_back1), table
    )
    return field_grad.reshape(1, XL, C, N, N), mode_grad


def solution(mesh):
    return jax.shard_map(
        per_device,
        mesh=mesh,
        in_specs=(
            P("dp", "space", None, None, None),
            P("dp", "space", None, None, None),
            P("space", None, None, None),
            P(),
            P(),
        ),
        out_specs=(P("dp", "space", None, None, None), P("space", "dp", None, None)),
        check_vma=False,
    )
```

```python
import functools
import math

import jax
import jax.numpy as jnp
import numpy as np
from jax import lax
from jax.experimental import pallas as pl
from jax.experimental.pallas import tpu as pltpu
from jax.sharding import PartitionSpec as P

BF = jnp.bfloat16
F32 = jnp.float32

C = 64
M = 16
N = 128
XL = 2
XC = XL * C
PAIRS = M * M
OWN = 4
GROUPS = 64
SLOPE_HEAD = 16
RESULT_HEADS = (32, 48)


def basis(length, count):
    points = np.arange(length)[:, None]
    order = np.arange(count)[None, :]
    freq = (order + 1) // 2
    phase = (points * freq % length).astype(np.float32) * np.float32(2.0 * math.pi / length)
    cosine = np.logical_or(order % 2 == 1, order == 0)
    table = np.where(cosine, np.cos(phase), np.sin(phase)) * np.float32(math.sqrt(2.0 / length))
    return table.astype(np.float32)


def split(table):
    high = table.astype(BF)
    return high, (table - high.astype(np.float32)).astype(BF)


def tables():
    base = basis(N, M)
    table_z = base.astype(BF)
    forward_y = np.kron(np.eye(2, dtype=np.float32), base.T)
    back_y = np.concatenate(split(base), axis=1)
    by_plane = base.reshape(GROUPS, XL, M)
    along_x = np.einsum("sxm,pq->xpmsq", by_plane, np.eye(OWN, dtype=np.float32)).reshape(XL * OWN * M, GROUPS * OWN)
    return dict(
        forward_y=forward_y.astype(BF),
        forward_y_half=(0.5 * forward_y).astype(BF),
        spread=np.kron(np.eye(C, dtype=np.float32), np.ones((ROWS, 1), np.float32)).astype(BF),
        back_y=back_y.astype(BF),
        forward_z=np.ascontiguousarray(table_z.T),
        along_x=np.stack(split(along_x)),
        back_x=np.stack(split(np.ascontiguousarray(along_x.T))),
    )


def y_modes(group, forward_y, scratch, row):
    block = jnp.concatenate(
        [jnp.concatenate(group[0:2], axis=0), jnp.concatenate(group[2:4], axis=0)], axis=1
    )
    modes = jnp.dot(forward_y, block, preferred_element_type=F32)
    scratch[pl.ds(row, 2 * M), :] = modes[:, :N]
    scratch[pl.ds(row + 2 * M, 2 * M), :] = modes[:, N:]


def z_modes(scratch, forward_z, modes, out_ref, sem):
    for a in range(M):
        part = scratch[pl.ds(a, XC, stride=M), :].astype(BF)
        modes[M * a : M * (a + 1), :] = lax.dot_general(
            forward_z, part, (((1,), (1,)), ((), ())), preferred_element_type=F32
        ).astype(BF)
    copy = pltpu.make_async_copy(modes, out_ref, sem)
    copy.start()
    return copy


def from_z_modes(modes, table_z, scratch):
    for a in range(M):
        scratch[pl.ds(a, XC, stride=M), :] = lax.dot_general(
            modes[M * a : M * (a + 1)], table_z, (((0,), (0,)), ((), ())), preferred_element_type=F32
        )


def from_y_modes(scratch, back_y, row):
    pair = jnp.concatenate(
        [scratch[pl.ds(row, M), :].astype(BF), scratch[pl.ds(row + M, M), :].astype(BF)], axis=1
    )
    return jnp.dot(back_y, jnp.concatenate([pair, pair], axis=0), preferred_element_type=F32)


def pieces(source, target, sems, cuts, first=0):
    return {
        low: pltpu.make_async_copy(
            source.at[pl.ds(low - first, high - low)], target.at[pl.ds(low, high - low)], sems.at[k]
        )
        for k, (low, high) in enumerate(zip(cuts, cuts[1:]))
    }


FIELD_CUTS = (0, 48, 96, 128)


def to_modes_kernel(
    field_ref, forward_y_ref, forward_z_ref, out_ref, held, scratch, modes, forward_y, forward_z, sems, small_sems
):
    small = [
        pltpu.make_async_copy(forward_y_ref, forward_y, small_sems.at[0]),
        pltpu.make_async_copy(forward_z_ref, forward_z, small_sems.at[1]),
    ]
    copies = pieces(field_ref, held, sems, FIELD_CUTS)
    for copy in (*small, *copies.values()):
        copy.start()
    for copy in small:
        copy.wait()
    for g in range(0, XC, 4):
        if g in copies:
            copies[g].wait()
        y_modes([held[g + j] for j in range(4)], forward_y[...], scratch, g * M)
    z_modes(scratch, forward_z[...], modes, out_ref, small_sems.at[2]).wait()


SLOPE_CUTS = (0, SLOPE_HEAD, 40, C, 96, 128)
SLOPE_OUT_CUTS = (0, 32, 64, 88, 104, 116, 128)
RESULT_CUTS = (0, RESULT_HEADS[0], C, 96, C + RESULT_HEADS[1], 128)
AHEAD = 2
BEHIND = 2


def ahead_of(product, count):
    ready = {}

    def take(at):
        for each in range(at, min(at + 2 * count + 2, XC), 2):
            if each not in ready:
                ready[each] = product(each)
        return ready[at]

    return take


def doubled_slope(pre, cot):
    root = math.sqrt(2.0 / math.pi)
    square = pre * pre
    tanh = jnp.tanh(pre * (root + (root * 0.044715) * square))
    outer = pre * (root + (root * 3 * 0.044715) * square)
    return (1.0 + tanh) * (1.0 + outer * (1.0 - tanh)) * cot


def slope_kernel(
    spatial_ref, table_z_ref, back_y_ref, forward_y_ref, point_head_ref, cot_head_ref,
    point0_ref, point1_ref, cot_ref, slope_ref, out_ref, spread, scratch, modes, point, cot, slope, sems, out_sem,
):
    point_copies = pieces(point0_ref, point, sems.at[0], SLOPE_CUTS[1:4])
    point_copies |= pieces(point1_ref, point, sems.at[1], SLOPE_CUTS[3:], C)
    cot_copies = pieces(cot_ref, cot, sems.at[2], SLOPE_CUTS[1:])
    slope_copies = pieces(slope, slope_ref, sems.at[3], SLOPE_OUT_CUTS)
    for low in SLOPE_CUTS[1:-1]:
        point_copies[low].start()
        cot_copies[low].start()
    from_z_modes(spatial_ref[...], table_z_ref[...], spread)
    spectral = ahead_of(lambda at: from_y_modes(spread, back_y_ref[...], at * M).astype(BF), AHEAD)
    waiting = []
    for first in range(0, XC, 4):
        if first in cot_copies:
            point_copies[first].wait()
            cot_copies[first].wait()
        point_at, cot_at = (point, cot) if first >= SLOPE_HEAD else (point_head_ref, cot_head_ref)
        group = []
        for at in range(first, first + 4, 2):
            both = spectral(at)
            for h in range(2):
                value = doubled_slope(both[:, N * h : N * (h + 1)] + point_at[at + h], cot_at[at + h])
                slope[at + h] = value
                group.append(value)
        waiting.append((group, first))
        if len(waiting) > BEHIND:
            group, row = waiting.pop(0)
            y_modes(group, forward_y_ref[...], scratch, row * M)
        for low, high in zip(SLOPE_OUT_CUTS, SLOPE_OUT_CUTS[1:]):
            if first + 4 == high:
                slope_copies[low].start()
    for group, row in waiting:
        y_modes(group, forward_y_ref[...], scratch, row * M)
    out_copy = z_modes(scratch, table_z_ref[...], modes, out_ref, out_sem)
    for copy in (*slope_copies.values(), out_copy):
        copy.wait()


def result_kernel(
    back_ref, table_z_ref, back_y_ref, both0_ref, both1_ref, both2_ref, both3_ref, head0_ref, head1_ref,
    point0_ref, point1_ref, out_ref, mode_grad_ref, spread, point, held, grads, total, sems, sem,
):
    point_copies = pieces(point0_ref, point, sems.at[0], (RESULT_HEADS[0], C))
    point_copies |= pieces(point1_ref, point, sems.at[1], (C + RESULT_HEADS[1], XC), C)
    out_copies = pieces(held, out_ref, sems.at[2], RESULT_CUTS)
    for copy in point_copies.values():
        copy.start()
    mode_gradient((both0_ref, both1_ref, both2_ref, both3_ref), grads, total)
    mode_copy = pltpu.make_async_copy(total, mode_grad_ref, sem)
    mode_copy.start()
    from_z_modes(back_ref[...], table_z_ref[...], spread)
    spectral = ahead_of(lambda at: from_y_modes(spread, back_y_ref[...], at * M), 1)
    for low, high in zip(RESULT_CUTS, RESULT_CUTS[1:]):
        if low in point_copies:
            point_copies[low].wait()
        for g in range(low, high, 2):
            both = spectral(g)
            for h in range(2):
                plane, channel = divmod(g + h, C)
                head = (head0_ref, head1_ref)[plane]
                other = head[channel] if channel < RESULT_HEADS[plane] else point[g + h]
                held[g + h] = (both[:, N * h : N * (h + 1)] + other.astype(F32)).astype(BF)
        out_copies[low].start()
    for copy in (*out_copies.values(), mode_copy):
        copy.wait()


def mode_gradient(samples, grads, out_ref):
    quarter = M // len(samples)
    own = lax.axis_index("dp") * quarter
    for s, ref in enumerate(samples):
        grads[s] = ref[...].astype(F32)
    lane = lax.broadcasted_iota(jnp.int32, (M, quarter * C), 1)
    row = lax.broadcasted_iota(jnp.int32, (M, quarter * C), 0)
    for p in range(OWN):
        rows = jnp.concatenate([grads[s, pl.ds(p * M + own, quarter), :] for s in range(len(samples))], axis=0)
        spectrum = jnp.concatenate([rows[:, :C]] * quarter, axis=1)
        spectrum = jnp.where(lane // C == row % quarter, spectrum, 0.0).astype(BF)
        out_ref[p] = lax.dot_general(
            spectrum, rows[:, C:].astype(BF), (((0,), (0,)), ((), ())), preferred_element_type=F32
        ).reshape(quarter, C, C)


ROWS = 8
WIDE = C * ROWS


def widen(weight_ref, spread_ref, wide, transposed, factor):
    rows = lax.dot_general(
        spread_ref[...], weight_ref[...], (((1,), (int(transposed),)), ((), ())), preferred_element_type=F32
    ).astype(BF)
    for k in range(0, WIDE, 128):
        every = lax.dot_general(
            rows[k : k + 128], spread_ref[...], (((1,), (1,)), ((), ())), preferred_element_type=F32
        )
        row = lax.broadcasted_iota(jnp.int32, (128, WIDE), 0)
        column = lax.broadcasted_iota(jnp.int32, (128, WIDE), 1)
        wide[k : k + 128, :] = jnp.where(row % ROWS == column % ROWS, every * factor, 0.0).astype(BF)


YB = 32
STEPS = N // YB


def fetch_rows(source, target, sems, count=YB):
    def copy(k):
        at = (slice(None), pl.ds(k * count, count))
        return pltpu.make_async_copy(source.at[at], target.at[at], sems.at[k])

    return copy


def point_rows(array, wide, bias, out, k, count=YB):
    size = 256
    for y in range(k * count, (k + 1) * count, 2 * ROWS):
        values = array[:, y : y + 2 * ROWS, :].astype(F32)
        block = jnp.concatenate(
            [values[:, ROWS * h : ROWS * (h + 1)].reshape(WIDE, N).astype(BF) for h in range(2)], axis=1
        )
        for at in range(0, WIDE, size):
            part = jnp.dot(wide[at : at + size, :], block, preferred_element_type=F32)
            pieces = []
            for h in range(2):
                piece = part[:, N * h : N * (h + 1)]
                if bias is not None:
                    piece = piece + bias[at : at + size, :]
                pieces.append(piece.reshape(size // ROWS, ROWS, N))
            out[at // ROWS : (at + size) // ROWS, y : y + 2 * ROWS, :] = jnp.concatenate(pieces, axis=1).astype(
                out.dtype
            )


def point_kernel(plane, weight_ref, spread_ref, bias_ref, *refs):
    refs, (array, out, bias, wide, sems, head_sem) = refs[:-6], refs[-6:]
    if plane:
        in_ref, out_ref = refs
    else:
        cot_ref, in_ref, out_ref, head_ref, cot_head_ref = refs
        head_copy = pltpu.make_async_copy(cot_ref.at[pl.ds(0, SLOPE_HEAD)], cot_head_ref, head_sem)
    copy = fetch_rows(in_ref.at[pl.ds(plane * C, C)], array, sems.at[0])
    out_copy = fetch_rows(out, out_ref, sems.at[1])
    for k in range(STEPS):
        copy(k).start()
    if not plane:
        head_copy.start()
    high = bias_ref[...].astype(BF)
    low = (bias_ref[...] - high.astype(F32)).astype(BF)
    bias[...] = sum(
        lax.dot_general(
            spread_ref[...], jnp.broadcast_to(part, (N, C)), (((1,), (1,)), ((), ())), preferred_element_type=F32
        )
        for part in (high, low)
    )
    widen(weight_ref, spread_ref, wide, True, 1.0)
    for k in range(STEPS):
        copy(k).wait()
        point_rows(array, wide, bias, out, k)
        out_copy(k).start()
    if not plane:
        head_ref[...] = out[:SLOPE_HEAD]
        head_copy.wait()
    for k in range(STEPS):
        out_copy(k).wait()


def point_back_kernel(plane, *refs):
    refs, (array, out, sems) = refs[:-3], refs[-3:]
    if plane:
        wide, in_ref, out_ref, head_ref = refs
    else:
        weight_ref, spread_ref, in_ref, out_ref, head_ref, wide = refs
    copy = fetch_rows(in_ref.at[pl.ds(plane * C, C)], array, sems.at[0])
    out_copy = fetch_rows(out, out_ref, sems.at[1])
    for k in range(STEPS):
        copy(k).start()
    if not plane:
        widen(weight_ref, spread_ref, wide, False, 0.5)
    for k in range(STEPS):
        copy(k).wait()
        point_rows(array, wide, None, out, k)
        out_copy(k).start()
    head_ref[...] = out[: RESULT_HEADS[plane]]
    for k in range(STEPS):
        out_copy(k).wait()


def x_modes(received, along_x):
    both = jnp.dot(along_x[0], received, preferred_element_type=F32)
    both += jnp.dot(along_x[1], received, preferred_element_type=F32)
    half = OWN * M
    lane = lax.broadcasted_iota(jnp.int32, (half, XC), 1)
    picked = jnp.where(lane < C, both[:half], both[half:])
    return picked + pltpu.roll(picked, C, 1)


def from_x_modes(twice, back_x):
    lane = lax.broadcasted_iota(jnp.int32, (OWN * M, XC), 1)
    stacked = jnp.concatenate([jnp.where(lane < C, twice, 0.0), jnp.where(lane < C, 0.0, twice)], axis=0)
    stacked = stacked.astype(BF)
    return jnp.dot(back_x[0], stacked, preferred_element_type=F32) + jnp.dot(
        back_x[1], stacked, preferred_element_type=F32
    )


def mix_kernel(received_ref, along_x_ref, back_x_ref, weight_ref, out_ref, spectrum_ref):
    spectrum = x_modes(received_ref[...], along_x_ref[...]).astype(BF)
    spectrum_ref[...] = spectrum
    lane = lax.broadcasted_iota(jnp.int32, (OWN * M, XC), 1)
    row = lax.broadcasted_iota(jnp.int32, (OWN * M, XC), 0) % M
    wide = spectrum.astype(F32)
    spread = jnp.concatenate(
        [jnp.where(lane // C + 2 * k == row, wide, 0.0).astype(BF) for k in range(M // 2)], axis=1
    )
    mixed = jnp.concatenate(
        [
            jnp.dot(spread[M * p : M * (p + 1)], weight_ref[p], preferred_element_type=F32)
            for p in range(OWN)
        ],
        axis=0,
    )
    twice = jnp.concatenate([mixed, mixed], axis=1)
    out_ref[...] = from_x_modes(twice, back_x_ref[...]).astype(out_ref.dtype)


def mix_back_kernel(received_ref, along_x_ref, back_x_ref, weight_ref, spectrum_ref, out_ref, both_ref):
    hat = x_modes(received_ref[...], along_x_ref[...]).astype(BF)
    lane = lax.broadcasted_iota(jnp.int32, (OWN * M, XC), 1)
    both_ref[...] = jnp.where(lane < C, spectrum_ref[...].astype(F32), hat.astype(F32)).astype(BF)
    lane = lax.broadcasted_iota(jnp.int32, (M, XC), 1)
    row = lax.broadcasted_iota(jnp.int32, (M, XC), 0)
    parts = []
    for p in range(OWN):
        every = lax.dot_general(
            hat[M * p : M * (p + 1), :C], weight_ref[p], (((1,), (1,)), ((), ())), preferred_element_type=F32
        )
        total = sum(
            jnp.where(lane // C + 2 * k == row, every[:, XC * k : XC * (k + 1)], 0.0) for k in range(M // 2)
        )
        parts.append(total + pltpu.roll(total, C, 1))
    out_ref[...] = from_x_modes(jnp.concatenate(parts, axis=0), back_x_ref[...]).astype(out_ref.dtype)


SMALL = pl.BlockSpec(memory_space=pltpu.VMEM)
LARGE = pl.BlockSpec(memory_space=pltpu.HBM)


def params(mib):
    return pltpu.CompilerParams(vmem_limit_bytes=mib * 1024 * 1024)


def cost(flops, size):
    return pl.CostEstimate(flops=flops, bytes_accessed=size, transcendentals=0)


ALL_BYTES = XC * N * N * 2
LARGE_OUT = pltpu.HBM((XC, N, N), BF)
PLANE_OUT = pltpu.HBM((C, N, N), BF)
MODES_OUT = pltpu.HBM((PAIRS, XC), BF)
MODES = pltpu.VMEM((PAIRS, XC), BF)
SMALL_OUT = jax.ShapeDtypeStruct((PAIRS, XC), BF)
OWN_OUT = jax.ShapeDtypeStruct((OWN * M, XC), BF)
WHOLE = pltpu.VMEM((XC, N, N), BF)
PLANE = pltpu.VMEM((C, N, N), BF)
SPREAD = pltpu.VMEM((XC * M, N), F32)


def large(array):
    return pltpu.with_memory_space_constraint(array, pltpu.HBM)


def sems(arrays, count):
    return pltpu.SemaphoreType.DMA((arrays, count))


def to_modes(field, table):
    small = (table["forward_y"], table["forward_z"])
    return pl.pallas_call(
        to_modes_kernel,
        in_specs=[LARGE] * 3,
        out_specs=LARGE,
        out_shape=MODES_OUT,
        scratch_shapes=[
            WHOLE, SPREAD, MODES, *[pltpu.VMEM(each.shape, BF) for each in small],
            pltpu.SemaphoreType.DMA((len(FIELD_CUTS) - 1,)), pltpu.SemaphoreType.DMA((3,)),
        ],
        compiler_params=params(40),
        cost_estimate=cost(XC * N * N * 128, ALL_BYTES),
        name="to_modes",
    )(large(field), *map(large, small))


def slopes(spatial, heads, points, cot, table):
    return pl.pallas_call(
        slope_kernel,
        in_specs=[SMALL] * 6 + [LARGE] * 3,
        out_specs=(LARGE, LARGE),
        out_shape=(LARGE_OUT, MODES_OUT),
        scratch_shapes=[SPREAD] * 2 + [MODES] + [WHOLE] * 3
        + [sems(4, len(SLOPE_OUT_CUTS)), pltpu.SemaphoreType.DMA],
        compiler_params=params(40),
        cost_estimate=cost(XC * N * N * 256, 3 * ALL_BYTES),
        name="slopes",
    )(
        spatial, table["forward_z"], table["back_y"], table["forward_y_half"], *heads,
        *map(large, points), large(cot),
    )


def result(back, samples, heads, points, table):
    return pl.pallas_call(
        result_kernel,
        in_specs=[SMALL] * 9 + [LARGE] * 2,
        out_specs=(LARGE, LARGE),
        out_shape=(LARGE_OUT, pltpu.HBM((OWN, M // 4, C, C), F32)),
        scratch_shapes=[
            SPREAD, WHOLE, WHOLE, pltpu.VMEM((4, OWN * M, XC), F32), pltpu.VMEM((OWN, M // 4, C, C), F32),
            sems(3, len(RESULT_CUTS)), pltpu.SemaphoreType.DMA,
        ],
        compiler_params=params(40),
        cost_estimate=cost(XC * N * N * 128, 2 * ALL_BYTES),
        name="result",
    )(back, table["forward_z"], table["back_y"], *samples, *heads, *map(large, points))


WIDENED = pltpu.VMEM((WIDE, WIDE), BF)
HALF = dict(
    compiler_params=params(40), cost_estimate=cost(C * N * N * 1024, ALL_BYTES), name="pointwise"
)


def pointwise(plane, weight, bias, array, table, cot=None):
    sources = ([] if cot is None else [cot]) + [array]
    heads = [pltpu.VMEM((SLOPE_HEAD, N, N), BF)] * (0 if plane else 2)
    return pl.pallas_call(
        functools.partial(point_kernel, plane),
        in_specs=[SMALL] * 3 + [LARGE] * len(sources),
        out_specs=[LARGE] + [SMALL] * len(heads),
        out_shape=[PLANE_OUT] + heads,
        scratch_shapes=[PLANE, PLANE, pltpu.VMEM((WIDE, N), F32), WIDENED, sems(2, STEPS), pltpu.SemaphoreType.DMA],
        **HALF,
    )(weight, table["spread"], bias.reshape(1, C), *map(large, sources))


def pointwise_back(plane, weights, array):
    kept = [pltpu.VMEM((RESULT_HEADS[plane], N, N), BF)] + [WIDENED] * (not plane)
    return pl.pallas_call(
        functools.partial(point_back_kernel, plane),
        in_specs=[SMALL] * len(weights) + [LARGE],
        out_specs=[LARGE] + [SMALL] * len(kept),
        out_shape=[PLANE_OUT] + kept,
        scratch_shapes=[PLANE, PLANE, sems(2, STEPS)],
        **HALF,
    )(*weights, large(array))


def mix(received, weight, table):
    return pl.pallas_call(
        mix_kernel,
        in_specs=[SMALL] * 4,
        out_specs=(SMALL, SMALL),
        out_shape=(SMALL_OUT, OWN_OUT),
        compiler_params=params(40),
        cost_estimate=cost(1 << 27, 1 << 21),
        name="mix",
    )(received, table["along_x"], table["back_x"], weight)


def mix_back(received, weight, spectrum, table):
    return pl.pallas_call(
        mix_back_kernel,
        in_specs=[SMALL] * 5,
        out_specs=(SMALL, SMALL),
        out_shape=(SMALL_OUT, OWN_OUT),
        compiler_params=params(40),
        cost_estimate=cost(1 << 27, 1 << 21),
        name="mix_back",
    )(received, table["along_x"], table["back_x"], weight, spectrum)


def exchange(array):
    cut = array.reshape(GROUPS, OWN, XC)
    return lax.all_to_all(cut, "space", split_axis=0, concat_axis=0, tiled=True).reshape(PAIRS, XC)


def over_samples(both):
    return [both] + [lax.ppermute(both, "dp", [(i, i ^ k) for i in range(4)]) for k in (2, 3, 1)]


def per_device(field, cotangent, mode_weight, point_weight, point_bias):
    table = {name: jnp.asarray(value) for name, value in tables().items()}
    sample = field.reshape(XC, N, N)
    cot = cotangent.reshape(XC, N, N)
    weight = mode_weight.reshape(OWN, M * C, C)

    modes, sample = lax.optimization_barrier((to_modes(sample, table), sample))
    received = exchange(modes)
    point0, *heads = pointwise(0, point_weight, point_bias, sample, table, cot)
    received, point0 = lax.optimization_barrier((received, point0))
    spatial, spectrum = mix(received, weight, table)
    later, spatial = lax.optimization_barrier((sample, spatial))
    received = exchange(spatial)
    (point1,) = pointwise(1, point_weight, point_bias, later, table)
    slope, grad_modes = slopes(received, heads, (point0, point1), cot, table)
    received = exchange(grad_modes)
    point_back0, head0, wide = pointwise_back(0, (point_weight, table["spread"]), slope)
    received, point_back0 = lax.optimization_barrier((received, point_back0))
    back, both = mix_back(received, weight, spectrum, table)
    later, back = lax.optimization_barrier((slope, back))
    back = exchange(back)
    point_back1, head1 = pointwise_back(1, (wide,), later)
    field_grad, mode_grad = result(
        back, over_samples(both), (head0, head1), (point_back0, point_back1), table
    )
    return field_grad.reshape(1, XL, C, N, N), mode_grad


def solution(mesh):
    return jax.shard_map(
        per_device,
        mesh=mesh,
        in_specs=(
            P("dp", "space", None, None, None),
            P("dp", "space", None, None, None),
            P("space", None, None, None),
            P(),
            P(),
        ),
        out_specs=(P("dp", "space", None, None, None), P("space", "dp", None, None)),
        check_vma=False,
    )
```

```python
import functools
import math

import jax
import jax.numpy as jnp
import numpy as np
from jax import lax
from jax.experimental import pallas as pl
from jax.experimental.pallas import tpu as pltpu
from jax.sharding import PartitionSpec as P

BF = jnp.bfloat16
F32 = jnp.float32

C = 64
M = 16
N = 128
XL = 2
XC = XL * C
PAIRS = M * M
OWN = 4
GROUPS = 64
SLOPE_HEAD = 16
RESULT_HEADS = (32, 48)


def basis(length, count):
    points = np.arange(length)[:, None]
    order = np.arange(count)[None, :]
    freq = (order + 1) // 2
    phase = (points * freq % length).astype(np.float32) * np.float32(2.0 * math.pi / length)
    cosine = np.logical_or(order % 2 == 1, order == 0)
    table = np.where(cosine, np.cos(phase), np.sin(phase)) * np.float32(math.sqrt(2.0 / length))
    return table.astype(np.float32)


def split(table):
    high = table.astype(BF)
    return high, (table - high.astype(np.float32)).astype(BF)


def tables():
    base = basis(N, M)
    table_z = base.astype(BF)
    forward_y = np.kron(np.eye(2, dtype=np.float32), base.T)
    back_y = np.concatenate(split(base), axis=1)
    by_plane = base.reshape(GROUPS, XL, M)
    along_x = np.einsum("sxm,pq->xpmsq", by_plane, np.eye(OWN, dtype=np.float32)).reshape(XL * OWN * M, GROUPS * OWN)
    return dict(
        forward_y=forward_y.astype(BF),
        forward_y_half=(0.5 * forward_y).astype(BF),
        spread=np.kron(np.eye(C, dtype=np.float32), np.ones((ROWS, 1), np.float32)).astype(BF),
        back_y=back_y.astype(BF),
        forward_z=np.ascontiguousarray(table_z.T),
        along_x=np.stack(split(along_x)),
        back_x=np.ascontiguousarray(along_x.T).astype(BF),
    )


def y_modes(group, forward_y, scratch, row):
    block = jnp.concatenate(
        [jnp.concatenate(group[0:2], axis=0), jnp.concatenate(group[2:4], axis=0)], axis=1
    )
    modes = jnp.dot(forward_y, block, preferred_element_type=F32)
    scratch[pl.ds(row, 2 * M), :] = modes[:, :N]
    scratch[pl.ds(row + 2 * M, 2 * M), :] = modes[:, N:]


def z_modes(scratch, forward_z, modes, out_ref, sem):
    for a in range(M):
        part = scratch[pl.ds(a, XC, stride=M), :].astype(BF)
        modes[M * a : M * (a + 1), :] = lax.dot_general(
            forward_z, part, (((1,), (1,)), ((), ())), preferred_element_type=F32
        ).astype(BF)
    copy = pltpu.make_async_copy(modes, out_ref, sem)
    copy.start()
    return copy


def from_z_modes(modes, table_z, scratch):
    for a in range(M):
        scratch[pl.ds(a, XC, stride=M), :] = lax.dot_general(
            modes[M * a : M * (a + 1)], table_z, (((0,), (0,)), ((), ())), preferred_element_type=F32
        )


def from_y_modes(scratch, back_y, row):
    pair = jnp.concatenate(
        [scratch[pl.ds(row, M), :].astype(BF), scratch[pl.ds(row + M, M), :].astype(BF)], axis=1
    )
    return jnp.dot(back_y, jnp.concatenate([pair, pair], axis=0), preferred_element_type=F32)


def pieces(source, target, sems, cuts, first=0):
    return {
        low: pltpu.make_async_copy(
            source.at[pl.ds(low - first, high - low)], target.at[pl.ds(low, high - low)], sems.at[k]
        )
        for k, (low, high) in enumerate(zip(cuts, cuts[1:]))
    }


FIELD_CUTS = (0, 48, 96, 128)


def to_modes_kernel(
    field_ref, forward_y_ref, forward_z_ref, out_ref, held, scratch, modes, forward_y, forward_z, sems, small_sems
):
    small = [
        pltpu.make_async_copy(forward_y_ref, forward_y, small_sems.at[0]),
        pltpu.make_async_copy(forward_z_ref, forward_z, small_sems.at[1]),
    ]
    copies = pieces(field_ref, held, sems, FIELD_CUTS)
    for copy in (*small, *copies.values()):
        copy.start()
    for copy in small:
        copy.wait()
    for g in range(0, XC, 4):
        if g in copies:
            copies[g].wait()
        y_modes([held[g + j] for j in range(4)], forward_y[...], scratch, g * M)
    z_modes(scratch, forward_z[...], modes, out_ref, small_sems.at[2]).wait()


SLOPE_CUTS = (0, SLOPE_HEAD, 40, C, 96, 128)
SLOPE_OUT_CUTS = (0, 32, 64, 88, 104, 116, 128)
RESULT_CUTS = (0, RESULT_HEADS[0], C, 96, C + RESULT_HEADS[1], 128)
AHEAD = 2
BEHIND = 2


def ahead_of(product, count):
    ready = {}

    def take(at):
        for each in range(at, min(at + 2 * count + 2, XC), 2):
            if each not in ready:
                ready[each] = product(each)
        return ready[at]

    return take


def doubled_slope(pre, cot):
    root = math.sqrt(2.0 / math.pi)
    square = pre * pre
    tanh = jnp.tanh(pre * (root + (root * 0.044715) * square))
    outer = pre * (root + (root * 3 * 0.044715) * square)
    return (1.0 + tanh) * (1.0 + outer * (1.0 - tanh)) * cot


def slope_kernel(
    spatial_ref, table_z_ref, back_y_ref, forward_y_ref, point_head_ref, cot_head_ref,
    point0_ref, point1_ref, cot_ref, slope_ref, out_ref, spread, scratch, modes, point, cot, slope, sems, out_sem,
):
    point_copies = pieces(point0_ref, point, sems.at[0], SLOPE_CUTS[1:4])
    point_copies |= pieces(point1_ref, point, sems.at[1], SLOPE_CUTS[3:], C)
    cot_copies = pieces(cot_ref, cot, sems.at[2], SLOPE_CUTS[1:])
    slope_copies = pieces(slope, slope_ref, sems.at[3], SLOPE_OUT_CUTS)
    for low in SLOPE_CUTS[1:-1]:
        point_copies[low].start()
        cot_copies[low].start()
    from_z_modes(spatial_ref[...], table_z_ref[...], spread)
    spectral = ahead_of(lambda at: from_y_modes(spread, back_y_ref[...], at * M).astype(BF), AHEAD)
    waiting = []
    for first in range(0, XC, 4):
        if first in cot_copies:
            point_copies[first].wait()
            cot_copies[first].wait()
        point_at, cot_at = (point, cot) if first >= SLOPE_HEAD else (point_head_ref, cot_head_ref)
        group = []
        for at in range(first, first + 4, 2):
            both = spectral(at)
            for h in range(2):
                value = doubled_slope(both[:, N * h : N * (h + 1)] + point_at[at + h], cot_at[at + h])
                slope[at + h] = value
                group.append(value)
        waiting.append((group, first))
        if len(waiting) > BEHIND:
            group, row = waiting.pop(0)
            y_modes(group, forward_y_ref[...], scratch, row * M)
        for low, high in zip(SLOPE_OUT_CUTS, SLOPE_OUT_CUTS[1:]):
            if first + 4 == high:
                slope_copies[low].start()
    for group, row in waiting:
        y_modes(group, forward_y_ref[...], scratch, row * M)
    out_copy = z_modes(scratch, table_z_ref[...], modes, out_ref, out_sem)
    for copy in (*slope_copies.values(), out_copy):
        copy.wait()


def result_kernel(
    back_ref, table_z_ref, back_y_ref, both0_ref, both1_ref, both2_ref, both3_ref, head0_ref, head1_ref,
    point0_ref, point1_ref, out_ref, mode_grad_ref, spread, point, held, grads, total, sems, sem,
):
    point_copies = pieces(point0_ref, point, sems.at[0], (RESULT_HEADS[0], C))
    point_copies |= pieces(point1_ref, point, sems.at[1], (C + RESULT_HEADS[1], XC), C)
    out_copies = pieces(held, out_ref, sems.at[2], RESULT_CUTS)
    for copy in point_copies.values():
        copy.start()
    mode_gradient((both0_ref, both1_ref, both2_ref, both3_ref), grads, total)
    mode_copy = pltpu.make_async_copy(total, mode_grad_ref, sem)
    mode_copy.start()
    from_z_modes(back_ref[...], table_z_ref[...], spread)
    spectral = ahead_of(lambda at: from_y_modes(spread, back_y_ref[...], at * M), 1)
    for low, high in zip(RESULT_CUTS, RESULT_CUTS[1:]):
        if low in point_copies:
            point_copies[low].wait()
        for g in range(low, high, 2):
            both = spectral(g)
            for h in range(2):
                plane, channel = divmod(g + h, C)
                head = (head0_ref, head1_ref)[plane]
                other = head[channel] if channel < RESULT_HEADS[plane] else point[g + h]
                held[g + h] = (both[:, N * h : N * (h + 1)] + other.astype(F32)).astype(BF)
        out_copies[low].start()
    for copy in (*out_copies.values(), mode_copy):
        copy.wait()


def mode_gradient(samples, grads, out_ref):
    quarter = M // len(samples)
    own = lax.axis_index("dp") * quarter
    for s, ref in enumerate(samples):
        grads[s] = ref[...].astype(F32)
    lane = lax.broadcasted_iota(jnp.int32, (M, quarter * C), 1)
    row = lax.broadcasted_iota(jnp.int32, (M, quarter * C), 0)
    for p in range(OWN):
        rows = jnp.concatenate([grads[s, pl.ds(p * M + own, quarter), :] for s in range(len(samples))], axis=0)
        spectrum = jnp.concatenate([rows[:, :C]] * quarter, axis=1)
        spectrum = jnp.where(lane // C == row % quarter, spectrum, 0.0).astype(BF)
        out_ref[p] = lax.dot_general(
            spectrum, rows[:, C:].astype(BF), (((0,), (0,)), ((), ())), preferred_element_type=F32
        ).reshape(quarter, C, C)


ROWS = 8
WIDE = C * ROWS


def widen(weight_ref, spread_ref, wide, transposed, factor):
    rows = lax.dot_general(
        spread_ref[...], weight_ref[...], (((1,), (int(transposed),)), ((), ())), preferred_element_type=F32
    ).astype(BF)
    for k in range(0, WIDE, 128):
        every = lax.dot_general(
            rows[k : k + 128], spread_ref[...], (((1,), (1,)), ((), ())), preferred_element_type=F32
        )
        row = lax.broadcasted_iota(jnp.int32, (128, WIDE), 0)
        column = lax.broadcasted_iota(jnp.int32, (128, WIDE), 1)
        wide[k : k + 128, :] = jnp.where(row % ROWS == column % ROWS, every * factor, 0.0).astype(BF)


YB = 32
STEPS = N // YB


def fetch_rows(source, target, sems, count=YB):
    def copy(k):
        at = (slice(None), pl.ds(k * count, count))
        return pltpu.make_async_copy(source.at[at], target.at[at], sems.at[k])

    return copy


def point_rows(array, wide, bias, out, k, count=YB):
    size = 256
    for y in range(k * count, (k + 1) * count, 2 * ROWS):
        values = array[:, y : y + 2 * ROWS, :].astype(F32)
        block = jnp.concatenate(
            [values[:, ROWS * h : ROWS * (h + 1)].reshape(WIDE, N).astype(BF) for h in range(2)], axis=1
        )
        for at in range(0, WIDE, size):
            part = jnp.dot(wide[at : at + size, :], block, preferred_element_type=F32)
            pieces = []
            for h in range(2):
                piece = part[:, N * h : N * (h + 1)]
                if bias is not None:
                    piece = piece + bias[at : at + size, :]
                pieces.append(piece.reshape(size // ROWS, ROWS, N))
            out[at // ROWS : (at + size) // ROWS, y : y + 2 * ROWS, :] = jnp.concatenate(pieces, axis=1).astype(
                out.dtype
            )


def point_kernel(plane, weight_ref, spread_ref, bias_ref, *refs):
    refs, (array, out, bias, wide, sems, head_sem) = refs[:-6], refs[-6:]
    if plane:
        in_ref, out_ref = refs
    else:
        cot_ref, in_ref, out_ref, head_ref, cot_head_ref = refs
        head_copy = pltpu.make_async_copy(cot_ref.at[pl.ds(0, SLOPE_HEAD)], cot_head_ref, head_sem)
    copy = fetch_rows(in_ref.at[pl.ds(plane * C, C)], array, sems.at[0])
    out_copy = fetch_rows(out, out_ref, sems.at[1])
    for k in range(STEPS):
        copy(k).start()
    if not plane:
        head_copy.start()
    high = bias_ref[...].astype(BF)
    low = (bias_ref[...] - high.astype(F32)).astype(BF)
    bias[...] = sum(
        lax.dot_general(
            spread_ref[...], jnp.broadcast_to(part, (N, C)), (((1,), (1,)), ((), ())), preferred_element_type=F32
        )
        for part in (high, low)
    )
    widen(weight_ref, spread_ref, wide, True, 1.0)
    for k in range(STEPS):
        copy(k).wait()
        point_rows(array, wide, bias, out, k)
        out_copy(k).start()
    if not plane:
        head_ref[...] = out[:SLOPE_HEAD]
        head_copy.wait()
    for k in range(STEPS):
        out_copy(k).wait()


def point_back_kernel(plane, *refs):
    refs, (array, out, sems) = refs[:-3], refs[-3:]
    if plane:
        wide, in_ref, out_ref, head_ref = refs
    else:
        weight_ref, spread_ref, in_ref, out_ref, head_ref, wide = refs
    copy = fetch_rows(in_ref.at[pl.ds(plane * C, C)], array, sems.at[0])
    out_copy = fetch_rows(out, out_ref, sems.at[1])
    for k in range(STEPS):
        copy(k).start()
    if not plane:
        widen(weight_ref, spread_ref, wide, False, 0.5)
    for k in range(STEPS):
        copy(k).wait()
        point_rows(array, wide, None, out, k)
        out_copy(k).start()
    head_ref[...] = out[: RESULT_HEADS[plane]]
    for k in range(STEPS):
        out_copy(k).wait()


def x_modes(received, along_x):
    both = jnp.dot(along_x[0], received, preferred_element_type=F32)
    both += jnp.dot(along_x[1], received, preferred_element_type=F32)
    half = OWN * M
    lane = lax.broadcasted_iota(jnp.int32, (half, XC), 1)
    picked = jnp.where(lane < C, both[:half], both[half:])
    return picked + pltpu.roll(picked, C, 1)


def from_x_modes(twice, back_x):
    lane = lax.broadcasted_iota(jnp.int32, (OWN * M, XC), 1)
    stacked = jnp.concatenate([jnp.where(lane < C, twice, 0.0), jnp.where(lane < C, 0.0, twice)], axis=0)
    stacked = stacked.astype(BF)
    return jnp.dot(back_x, stacked, preferred_element_type=F32)


def mix_kernel(received_ref, along_x_ref, back_x_ref, weight_ref, out_ref, spectrum_ref):
    spectrum = x_modes(received_ref[...], along_x_ref[...]).astype(BF)
    spectrum_ref[...] = spectrum
    lane = lax.broadcasted_iota(jnp.int32, (OWN * M, XC), 1)
    row = lax.broadcasted_iota(jnp.int32, (OWN * M, XC), 0) % M
    wide = spectrum.astype(F32)
    spread = jnp.concatenate(
        [jnp.where(lane // C + 2 * k == row, wide, 0.0).astype(BF) for k in range(M // 2)], axis=1
    )
    mixed = jnp.concatenate(
        [
            jnp.dot(spread[M * p : M * (p + 1)], weight_ref[p], preferred_element_type=F32)
            for p in range(OWN)
        ],
        axis=0,
    )
    twice = jnp.concatenate([mixed, mixed], axis=1)
    out_ref[...] = from_x_modes(twice, back_x_ref[...]).astype(out_ref.dtype)


def mix_back_kernel(received_ref, along_x_ref, back_x_ref, weight_ref, spectrum_ref, out_ref, both_ref):
    hat = x_modes(received_ref[...], along_x_ref[...]).astype(BF)
    lane = lax.broadcasted_iota(jnp.int32, (OWN * M, XC), 1)
    both_ref[...] = jnp.where(lane < C, spectrum_ref[...].astype(F32), hat.astype(F32)).astype(BF)
    lane = lax.broadcasted_iota(jnp.int32, (M, XC), 1)
    row = lax.broadcasted_iota(jnp.int32, (M, XC), 0)
    parts = []
    for p in range(OWN):
        every = lax.dot_general(
            hat[M * p : M * (p + 1), :C], weight_ref[p], (((1,), (1,)), ((), ())), preferred_element_type=F32
        )
        total = sum(
            jnp.where(lane // C + 2 * k == row, every[:, XC * k : XC * (k + 1)], 0.0) for k in range(M // 2)
        )
        parts.append(total + pltpu.roll(total, C, 1))
    out_ref[...] = from_x_modes(jnp.concatenate(parts, axis=0), back_x_ref[...]).astype(out_ref.dtype)


SMALL = pl.BlockSpec(memory_space=pltpu.VMEM)
LARGE = pl.BlockSpec(memory_space=pltpu.HBM)


def params(mib):
    return pltpu.CompilerParams(vmem_limit_bytes=mib * 1024 * 1024)


def cost(flops, size):
    return pl.CostEstimate(flops=flops, bytes_accessed=size, transcendentals=0)


ALL_BYTES = XC * N * N * 2
LARGE_OUT = pltpu.HBM((XC, N, N), BF)
PLANE_OUT = pltpu.HBM((C, N, N), BF)
MODES_OUT = pltpu.HBM((PAIRS, XC), BF)
MODES = pltpu.VMEM((PAIRS, XC), BF)
SMALL_OUT = jax.ShapeDtypeStruct((PAIRS, XC), BF)
OWN_OUT = jax.ShapeDtypeStruct((OWN * M, XC), BF)
WHOLE = pltpu.VMEM((XC, N, N), BF)
PLANE = pltpu.VMEM((C, N, N), BF)
SPREAD = pltpu.VMEM((XC * M, N), F32)


def large(array):
    return pltpu.with_memory_space_constraint(array, pltpu.HBM)


def sems(arrays, count):
    return pltpu.SemaphoreType.DMA((arrays, count))


def to_modes(field, table):
    small = (table["forward_y"], table["forward_z"])
    return pl.pallas_call(
        to_modes_kernel,
        in_specs=[LARGE] * 3,
        out_specs=LARGE,
        out_shape=MODES_OUT,
        scratch_shapes=[
            WHOLE, SPREAD, MODES, *[pltpu.VMEM(each.shape, BF) for each in small],
            pltpu.SemaphoreType.DMA((len(FIELD_CUTS) - 1,)), pltpu.SemaphoreType.DMA((3,)),
        ],
        compiler_params=params(40),
        cost_estimate=cost(XC * N * N * 128, ALL_BYTES),
        name="to_modes",
    )(large(field), *map(large, small))


def slopes(spatial, heads, points, cot, table):
    return pl.pallas_call(
        slope_kernel,
        in_specs=[SMALL] * 6 + [LARGE] * 3,
        out_specs=(LARGE, LARGE),
        out_shape=(LARGE_OUT, MODES_OUT),
        scratch_shapes=[SPREAD] * 2 + [MODES] + [WHOLE] * 3
        + [sems(4, len(SLOPE_OUT_CUTS)), pltpu.SemaphoreType.DMA],
        compiler_params=params(40),
        cost_estimate=cost(XC * N * N * 256, 3 * ALL_BYTES),
        name="slopes",
    )(
        spatial, table["forward_z"], table["back_y"], table["forward_y_half"], *heads,
        *map(large, points), large(cot),
    )


def result(back, samples, heads, points, table):
    return pl.pallas_call(
        result_kernel,
        in_specs=[SMALL] * 9 + [LARGE] * 2,
        out_specs=(LARGE, LARGE),
        out_shape=(LARGE_OUT, pltpu.HBM((OWN, M // 4, C, C), F32)),
        scratch_shapes=[
            SPREAD, WHOLE, WHOLE, pltpu.VMEM((4, OWN * M, XC), F32), pltpu.VMEM((OWN, M // 4, C, C), F32),
            sems(3, len(RESULT_CUTS)), pltpu.SemaphoreType.DMA,
        ],
        compiler_params=params(40),
        cost_estimate=cost(XC * N * N * 128, 2 * ALL_BYTES),
        name="result",
    )(back, table["forward_z"], table["back_y"], *samples, *heads, *map(large, points))


WIDENED = pltpu.VMEM((WIDE, WIDE), BF)
HALF = dict(
    compiler_params=params(40), cost_estimate=cost(C * N * N * 1024, ALL_BYTES), name="pointwise"
)


def pointwise(plane, weight, bias, array, table, cot=None):
    sources = ([] if cot is None else [cot]) + [array]
    heads = [pltpu.VMEM((SLOPE_HEAD, N, N), BF)] * (0 if plane else 2)
    return pl.pallas_call(
        functools.partial(point_kernel, plane),
        in_specs=[SMALL] * 3 + [LARGE] * len(sources),
        out_specs=[LARGE] + [SMALL] * len(heads),
        out_shape=[PLANE_OUT] + heads,
        scratch_shapes=[PLANE, PLANE, pltpu.VMEM((WIDE, N), F32), WIDENED, sems(2, STEPS), pltpu.SemaphoreType.DMA],
        **HALF,
    )(weight, table["spread"], bias.reshape(1, C), *map(large, sources))


def pointwise_back(plane, weights, array):
    kept = [pltpu.VMEM((RESULT_HEADS[plane], N, N), BF)] + [WIDENED] * (not plane)
    return pl.pallas_call(
        functools.partial(point_back_kernel, plane),
        in_specs=[SMALL] * len(weights) + [LARGE],
        out_specs=[LARGE] + [SMALL] * len(kept),
        out_shape=[PLANE_OUT] + kept,
        scratch_shapes=[PLANE, PLANE, sems(2, STEPS)],
        **HALF,
    )(*weights, large(array))


def mix(received, weight, table):
    return pl.pallas_call(
        mix_kernel,
        in_specs=[SMALL] * 4,
        out_specs=(SMALL, SMALL),
        out_shape=(SMALL_OUT, OWN_OUT),
        compiler_params=params(40),
        cost_estimate=cost(1 << 27, 1 << 21),
        name="mix",
    )(received, table["along_x"], table["back_x"], weight)


def mix_back(received, weight, spectrum, table):
    return pl.pallas_call(
        mix_back_kernel,
        in_specs=[SMALL] * 5,
        out_specs=(SMALL, SMALL),
        out_shape=(SMALL_OUT, OWN_OUT),
        compiler_params=params(40),
        cost_estimate=cost(1 << 27, 1 << 21),
        name="mix_back",
    )(received, table["along_x"], table["back_x"], weight, spectrum)


def exchange(array):
    cut = array.reshape(GROUPS, OWN, XC)
    return lax.all_to_all(cut, "space", split_axis=0, concat_axis=0, tiled=True).reshape(PAIRS, XC)


def over_samples(both):
    return [both] + [lax.ppermute(both, "dp", [(i, i ^ k) for i in range(4)]) for k in (2, 3, 1)]


def per_device(field, cotangent, mode_weight, point_weight, point_bias):
    table = {name: jnp.asarray(value) for name, value in tables().items()}
    sample = field.reshape(XC, N, N)
    cot = cotangent.reshape(XC, N, N)
    weight = mode_weight.reshape(OWN, M * C, C)

    modes, sample = lax.optimization_barrier((to_modes(sample, table), sample))
    received = exchange(modes)
    point0, *heads = pointwise(0, point_weight, point_bias, sample, table, cot)
    received, point0 = lax.optimization_barrier((received, point0))
    spatial, spectrum = mix(received, weight, table)
    later, spatial = lax.optimization_barrier((sample, spatial))
    received = exchange(spatial)
    (point1,) = pointwise(1, point_weight, point_bias, later, table)
    slope, grad_modes = slopes(received, heads, (point0, point1), cot, table)
    received = exchange(grad_modes)
    point_back0, head0, wide = pointwise_back(0, (point_weight, table["spread"]), slope)
    received, point_back0 = lax.optimization_barrier((received, point_back0))
    back, both = mix_back(received, weight, spectrum, table)
    later, back = lax.optimization_barrier((slope, back))
    back = exchange(back)
    point_back1, head1 = pointwise_back(1, (wide,), later)
    field_grad, mode_grad = result(
        back, over_samples(both), (head0, head1), (point_back0, point_back1), table
    )
    return field_grad.reshape(1, XL, C, N, N), mode_grad


def solution(mesh):
    return jax.shard_map(
        per_device,
        mesh=mesh,
        in_specs=(
            P("dp", "space", None, None, None),
            P("dp", "space", None, None, None),
            P("space", None, None, None),
            P(),
            P(),
        ),
        out_specs=(P("dp", "space", None, None, None), P("space", "dp", None, None)),
        check_vma=False,
    )
```
